128 devices in a mesh: bin: 16 (over x, y_hi, core), dist: 8 (over z, y_lo).
Axes of the slice: x: 4, y: 4 (y_hi: 2, y_lo: 2; y = y_hi * 2 + y_lo), z: 4, core: 2. Of those that a mesh axis runs over, the one named last changes fastest.
Arguments:
- wavefuncs: bfloat16 [1536, 512], P('bin', 'dist'), may hold values from -6 to 6
- kernel: bfloat16 [512, 512], P(None, 'dist'), may hold values from -0.25 to 0.25
- labels: int32 [1536], P('bin'), may hold values from 0 to 7
- row_tiles: int32 [1024], P('bin'), may hold values from 0 to 2
- col_tiles: int32 [1024], P('bin'), may hold values from 0 to 47
- owners: int32 [1024, 1], P('bin'), may hold values from 0 to 15; in each aligned block of 64 rows (0 to 63, 64 to 127, ...) at most 8 rows name the same one
Outputs:
- owned_tiles: bfloat16 [2048, 512, 1024], P('bin', 'dist')
The draws below stay inside these ranges and needn't reach their ends.
Inputs may be any that keep to these rules, and one draw needn't show every extreme that they name: `owners`: among the 64 entries of one sender no owner appears more than 8 times, and some owner appears exactly 8 times.
All inputs are finite; a program needn't handle non-finite values.
Results may differ from the reference program's by a relative error of at most 0.005.
Values may be sent and summed in bfloat16 or wider, within the bound.
A program may use at most 128 MiB of HBM per device.

```python
import math
import jax
import jax.numpy as jnp
import numpy as np
from jax import lax

R = 512
RDIST = 512
TB = 32
LMAX = 8
SEL = 64
CHANNELS = 1536
TPB = 3
NT = 48
CAP = 8
N_BIN = 16


def place_ends(values, stream_key, low, high):
    extent = values.shape
    index_at = [jax.random.randint(jax.random.fold_in(stream_key, axis), (), 0, extent[axis]) for axis in range(len(extent))]
    values = values.at[tuple(index_at)].set(low)
    longest = extent.index(max(extent))
    index_at[longest] = (index_at[longest] + 1) % extent[longest]
    return values.at[tuple(index_at)].set(high)


def block_levels(stream_key, shape, split, smallest, largest):
    gain, own = 1.0, jax.random.fold_in(stream_key, 6)
    for axis_at, blocks in split:
        heights = jnp.exp(jax.random.uniform(jax.random.fold_in(own, axis_at), (blocks,), jnp.float32, smallest / len(split), largest / len(split)))
        gain = gain * jnp.repeat(heights, shape[axis_at] // blocks).reshape([-1 if axis == axis_at else 1 for axis in range(len(shape))])
    return gain


def deal_out(own_key, own, number, rows, number_of, top, bound, slope):
    ranking = jax.random.permutation(own_key, number_of)
    packed, ordinary = load_shares(number_of, rows * top, bound, slope, True), load_shares(number_of, rows * top, bound, slope, False)
    places = jnp.arange(number_of)

    def named(sizes, turn):
        used = int((sizes > 0).sum())
        fixed = max(1, used // 4)
        moved = fixed + (places - fixed + turn * (used - fixed)) % max(1, number_of - fixed)
        return jnp.zeros((number_of,), jnp.int32).at[ranking[jnp.where(places < fixed, places, moved)]].set(jnp.asarray(sizes, jnp.int32))

    sizes = jnp.where(number % 4 == 0, named(packed, number // 4), named(ordinary, number - number // 4 - 1))
    mixed = jax.random.permutation(jax.random.fold_in(own, 3), number_of)
    giver, receiver = mixed[0:number_of // 2 * 2:2], mixed[1:number_of // 2 * 2:2]
    slack = jnp.minimum(sizes[giver] - 1, bound - sizes[receiver]) // 2
    slack = jnp.where((giver == ranking[0]) | (receiver == ranking[0]) | (sizes[receiver] == 0), 0, jnp.maximum(slack, 0))
    moved = jax.random.randint(jax.random.fold_in(own, 4), (number_of // 2,), 0, 1 << 20) % (slack + 1)
    sizes = sizes.at[giver].add(-moved).at[receiver].add(moved)
    items = jnp.searchsorted(jnp.cumsum(sizes), jnp.arange(rows * top), side="right").astype(jnp.int32)
    grid = items.reshape(top, rows).T
    grid = grid[jax.random.permutation(jax.random.fold_in(own, 1), rows)]
    turn = jax.random.randint(jax.random.fold_in(own, 2), (rows, 1), 0, top)
    return jnp.take_along_axis(grid, (jnp.arange(top)[None, :] + turn) % top, axis=1)


def load_shares(count, total, most, skew, full):
    portions = [(1 << 20) // math.isqrt(grade ** skew) + 1 for grade in range(1, count + 1)]
    largest = most if full else min(most, max(-(-total // count), total * portions[0] // sum(portions)))
    least = 1 if total - largest >= count - 1 else 0
    counts, spare = [largest] + [least] * (count - 1), total - largest - least * (count - 1)
    while spare > 0:
        free = [i for i in range(1, count) if counts[i] < largest] or [i for i in range(1, count) if counts[i] < most]
        whole, left = sum([portions[i] for i in free]), spare
        for i in free:
            addition = min(most - counts[i], max(1, left * portions[i] // whole), spare)
            counts[i] = counts[i] + addition
            spare = spare - addition
    return np.array(counts)


def centred(own_key, extent, width, bound, cuts=(), kind=jnp.bfloat16):
    entries = jax.random.normal(own_key, extent, jnp.float32) * width
    if len(cuts) > 0:
        entries = block_levels(own_key, extent, cuts, -0.22, 0.18) * entries
    return jnp.clip(entries, min=-bound, max=bound).astype(kind)


def setup_inputs(seed: int = 0) -> dict:
    key_list = jax.random.split(jax.random.key(seed), 7)
    wavefuncs = centred(key_list[0], (CHANNELS, R), 1.0, 6.0, ((0, 16), (1, 8)))
    kernel = centred(key_list[1], (R, RDIST), R ** -0.5, 0.25, ((1, 8),))
    labels = place_ends(jax.random.randint(key_list[2], (CHANNELS,), 0, LMAX), jax.random.fold_in(key_list[2], 1), 0, LMAX - 1).astype(jnp.int32)
    row_tiles = place_ends(jax.random.randint(key_list[3], (N_BIN * SEL,), 0, TPB), jax.random.fold_in(key_list[3], 1), 0, TPB - 1).astype(jnp.int32)
    col_tiles = place_ends(jax.random.randint(key_list[4], (N_BIN * SEL,), 0, NT), jax.random.fold_in(key_list[4], 1), 0, NT - 1).astype(jnp.int32)
    owners_keys = jax.random.split(jax.random.fold_in(key_list[5], 1), (N_BIN * SEL) // SEL)
    owners_turns = jax.random.permutation(jax.random.fold_in(key_list[5], 3), (N_BIN * SEL) // SEL)
    owners = jax.vmap(lambda own, number: deal_out(jax.random.fold_in(key_list[5], 2), own, number, SEL, N_BIN, 1, 2 * SEL // N_BIN, 2))(owners_keys, owners_turns).reshape((N_BIN * SEL, 1))
    return dict(wavefuncs=wavefuncs, kernel=kernel, labels=labels, row_tiles=row_tiles, col_tiles=col_tiles, owners=owners)


def angular(left_l, right_l):
    left_f = left_l.astype(jnp.float32)[..., :, None]
    right_f = right_l.astype(jnp.float32)[..., None, :]
    return jnp.sqrt((2.0 * left_f + 1.0) * (2.0 * right_f + 1.0)) / (LMAX * (1.0 + jnp.abs(left_f - right_f)))

def tile_forms(row_wave, col_wave, row_label, col_label, kernel):
    product = jnp.einsum('kar,kbr->krab', row_wave.astype(jnp.float32), col_wave.astype(jnp.float32))
    pair_bf = (product * angular(row_label, col_label)[:, None]).astype(jnp.bfloat16)
    pair_bf = pair_bf.reshape(pair_bf.shape[0], pair_bf.shape[1], -1)
    return jnp.einsum('rd,krq->kdq', kernel.astype(jnp.float32), pair_bf.astype(jnp.float32)).astype(jnp.bfloat16)

def reference(wavefuncs, kernel, labels, row_tiles, col_tiles, owners):
    tile_wave = wavefuncs.reshape(NT, TB, R)
    tile_label = labels.reshape(NT, TB)
    output = jnp.zeros((N_BIN * N_BIN * CAP, RDIST, TB * TB), jnp.bfloat16)
    owner_ids = jnp.arange(N_BIN, dtype=jnp.int32)
    for sender in range(N_BIN):
        row_index = row_tiles[sender * SEL:(sender + 1) * SEL] + sender * TPB
        col_index = col_tiles[sender * SEL:(sender + 1) * SEL]
        owner_list = owners[sender * SEL:(sender + 1) * SEL, 0]
        onehot = (owner_list[:, None] == owner_ids[None, :]).astype(jnp.int32)
        slot_rank = lax.optimization_barrier(jnp.sum((jnp.cumsum(onehot, axis=0) - onehot) * onehot, axis=1))
        target_row = owner_list * (N_BIN * CAP) + sender * CAP + slot_rank

        def block_fn(pieces):
            row_piece, col_piece = pieces
            return tile_forms(tile_wave[row_piece], tile_wave[col_piece], tile_label[row_piece], tile_label[col_piece], kernel)
        tile_out = lax.map(block_fn, (row_index.reshape(-1, 8), col_index.reshape(-1, 8)))
        output = output.at[target_row].set(tile_out.reshape(SEL, RDIST, TB * TB))
    return output
```

```python
import functools
import jax
import jax.numpy as jnp
from jax import lax
from jax.experimental import pallas as pl
from jax.experimental.pallas import tpu as pltpu
from jax.sharding import PartitionSpec as P

D = 64
RPT = 3
CAP = 8
NS = 16
BF = jnp.bfloat16
F32 = jnp.float32
MESH = pl.DeviceIdType.MESH


def gather_kernel(wave, kern, labels, rows, cols, owners, b0, b1, b2, meta, kt,
                  table, z_send, z_recv, m_send, m_recv, c_send, c_recv):
    own, own_d = lax.axis_index("bin"), lax.axis_index("dist")
    x, yh, core = own // 4, (own // 2) % 2, own % 2
    z, yl = own_d // 2, own_d % 2
    y = yh * 2 + yl
    other = 1 - core

    def chip(px, py, pz, pc):
        return (px * 4 + (py // 2) * 2 + pc, pz * 2 + py % 2)

    def up(v, o):
        return (v + o) % 4

    barrier = pltpu.get_barrier_semaphore()
    peers = [((own + k) % NS, own_d) for k in range(1, NS)]
    peers += [chip(x, y, up(z, o), core) for o in (1, 2, 3)]
    peers += [chip(x, up(y, o), z, core) for o in (1, 3)]
    for peer in peers:
        pl.semaphore_signal(barrier, inc=1, device_id=peer, device_id_type=MESH)

    for rt, b in enumerate((b0, b1, b2)):
        part = jnp.concatenate(
            [wave[rt * 32 : rt * 32 + 16, :], wave[rt * 32 + 16 : rt * 32 + 32, :]], axis=1
        )
        if rt == 0:
            b[core, x, y, z] = part
        elif rt == 1:
            b[core, z, x, y] = part
        else:
            b[core, y, z, x] = part

    eye = lax.broadcasted_iota(jnp.int32, (64, 64), 0) == lax.broadcasted_iota(jnp.int32, (64, 64), 1)
    before = lax.broadcasted_iota(jnp.int32, (64, 64), 0) < lax.broadcasted_iota(jnp.int32, (64, 64), 1)

    def column(row):
        return jnp.sum(jnp.where(eye, jnp.broadcast_to(row, (64, 64)), 0), axis=1, keepdims=True)

    own_c = jnp.broadcast_to(owners[...], (64, 64))
    own_r = jnp.sum(jnp.where(eye, own_c, 0), axis=0, keepdims=True)
    rt_r, col_r = rows[...], cols[...]
    rt_c = jnp.broadcast_to(column(rt_r), (64, 64))
    same = (own_c == own_r) & before
    slot_r = jnp.sum(jnp.where(same, 1, 0), axis=0, keepdims=True)
    rank_r = jnp.sum(jnp.where(same & (rt_c == rt_r), 1, 0), axis=0, keepdims=True)
    third = lax.shift_right_logical(col_r * 171, 9)
    tile_r = (col_r - 3 * third) * 16 + third
    key_c = column(rt_r * 8 + rank_r)
    code_c = column(1 + tile_r * 8 + slot_r)
    lane64 = lax.broadcasted_iota(jnp.int32, (64, 128), 1)
    lane1 = lax.broadcasted_iota(jnp.int32, (1, 128), 1)
    spread = jnp.where(lane64 == key_c, jnp.broadcast_to(code_c, (64, 128)), 0)
    label_row = labels[...]
    for o in range(NS):
        mine = jnp.where(owners[...] == o, spread, 0)
        table[o] = jnp.where(lane1 < 32, jnp.sum(mine, axis=0, keepdims=True), label_row)

    meta[own] = table[own]

    pl.semaphore_wait(barrier, len(peers))

    def copy(src, dst, send, recv, device):
        return pltpu.make_async_remote_copy(
            src_ref=src, dst_ref=dst, send_sem=send, recv_sem=recv, device_id=device, device_id_type=MESH
        )

    sent = []

    def block(rt, stage, v, c):
        if rt == 0:
            return (b0.at[c, x, y, v], b0.at[c, x, v], b0.at[c, v])[stage]
        if rt == 1:
            return (b1.at[c, z, x, v], b1.at[c, z, v], b1.at[c, v])[stage]
        return (b2.at[c, y, z, v], b2.at[c, y, v], b2.at[c, v])[stage]

    def place(rt, stage):
        axis = ("zyx", "yxz", "xzy")[rt][stage]
        return {"x": x, "y": y, "z": z}[axis], axis

    def device(axis, v):
        return chip(v if axis == "x" else x, v if axis == "y" else y, v if axis == "z" else z, core)

    def push(rt, stage):
        at, axis = place(rt, stage)
        for o in (1, 3, 2):
            cp = copy(block(rt, stage, at, core), block(rt, stage, at, core),
                      z_send.at[rt, stage, o - 1], z_recv.at[rt, stage, o - 1], device(axis, up(at, o)))
            cp.start()
            sent.append(cp)

    def landed(rt, stage, o):
        at, axis = place(rt, stage)
        v = up(at, 4 - o)
        copy(block(rt, stage, v, core), block(rt, stage, v, core),
             z_send.at[rt, stage, o - 1], z_recv.at[rt, stage, o - 1], device(axis, v)).wait_recv()
        return v

    def across(rt, k, v, c):
        return copy(block(rt, 2, v, c), block(rt, 2, v, c), c_send.at[rt, k], c_recv.at[rt, k], chip(x, y, z, other))

    for rt in range(RPT):
        push(rt, 0)
    for k in range(1, NS):
        to = (own + k) % NS
        cp = copy(table.at[to], meta.at[own], m_send.at[k], m_recv.at[k], (to, own_d))
        cp.start()
        sent.append(cp)
    kt[...] = kern[...].astype(F32).T.astype(BF)
    for rt in range(RPT):
        for o in (1, 3, 2):
            landed(rt, 0, o)
        push(rt, 1)
    for rt in range(RPT):
        for o in (1, 3, 2):
            landed(rt, 1, o)
        push(rt, 2)
        cp = across(rt, 0, place(rt, 2)[0], core)
        cp.start()
        sent.append(cp)
    for o in (1, 3, 2):
        for rt in range(RPT):
            v = landed(rt, 2, o)
            cp = across(rt, o, v, core)
            cp.start()
            sent.append(cp)
    for k in range(1, NS):
        at = (own + NS - k) % NS
        copy(table.at[at], meta.at[at], m_send.at[k], m_recv.at[k], (at, own_d)).wait_recv()
    for o in (0, 1, 3, 2):
        for rt in range(RPT):
            across(rt, o, up(place(rt, 2)[0], (4 - o) % 4), other).wait_recv()
    for cp in sent:
        cp.wait_send()


def swap_blocks(lane, x):
    half=lane<64
    even=(lane//32)%2==0
    def cross(p,q,shift,mask):
        return jnp.where(mask,p,pltpu.roll(q,shift,1)), jnp.where(mask,pltpu.roll(p,128-shift,1),q)
    a0,a2=cross(x[0],x[2],64,half)
    a1,a3=cross(x[1],x[3],64,half)
    y0,y1=cross(a0,a1,32,even)
    y2,y3=cross(a2,a3,32,even)
    return y0,y1,y2,y3

def forms_kernel(msm, mv, kt_ref, b0, b1, b2, out, W, OUT, S1, ANG, LT, sem):
    lane16=lax.broadcasted_iota(jnp.int32,(16,128),1)
    lane=lax.broadcasted_iota(jnp.int32,(64,128),1)
    lo=lane16<64
    for rt,b in enumerate((b0,b1,b2)):
        for x in range(4):
            for yh in range(2):
                for c in range(2):
                    s=x*4+yh*2+c
                    for z in range(4):
                        def at(yl):
                            y=yh*2+yl
                            return b[c,x,y,z] if rt==0 else (b[c,z,x,y] if rt==1 else b[c,y,z,x])
                        p,q=at(0),at(1)
                        W[rt*16+s,0:16,z*128:(z+1)*128]=jnp.concatenate([p[:,:64],q[:,:64]],axis=1)
                        W[rt*16+s,16:32,z*128:(z+1)*128]=jnp.concatenate([p[:,64:],q[:,64:]],axis=1)
    m=mv[...].astype(F32).reshape(16,128)
    rolls=[m]+[pltpu.roll(m,32*k,1) for k in (1,2,3)]
    for rt in range(RPT):
        acc=rolls[(0-rt-1)%4]
        for g in (1,2,3):
            acc=jnp.where(lane16//32==g,rolls[(g-rt-1)%4],acc)
        LT[rt]=acc

    def sender(s, accs, first):
        buf=lax.rem(s,2)
        kt=kt_ref[...]
        dests=[]
        for rt in range(RPT):
            tau=[];dst=[]
            for n in range(CAP):
                code=msm[s,0,rt*8+n]
                ok=code>0
                cm=jnp.maximum(code-1,0)
                tau.append(cm>>3)
                dst.append(jnp.where(ok,cm&7,8))
            dests.append((tau,dst))
        eye=(lax.broadcasted_iota(jnp.int32,(32,128),1)==lax.broadcasted_iota(jnp.int32,(32,128),0))
        for rt in range(RPT):
            tau,_=dests[rt]
            lrow=LT[rt,pl.ds(s,1),:]
            li=jnp.sum(jnp.where(eye,jnp.broadcast_to(lrow,(32,128)),0.0),axis=1,keepdims=True)
            li=jnp.broadcast_to(li,(32,128))
            for h in range(2):
                lj=None
                for g in range(4):
                    t=tau[h*4+g]
                    row=LT[t>>4,pl.ds(t&15,1),:]
                    lj=row if lj is None else jnp.where(lane[0:1]//32==g,row,lj)
                lj=jnp.broadcast_to(lj,(32,128))
                ANG[rt,:,h*128:(h+1)*128]=jnp.sqrt((2.0*li+1.0)*(2.0*lj+1.0))/(8.0*(1.0+jnp.abs(li-lj)))
        def push(rt):
            cols=jnp.concatenate([W[dests[rt][0][n]] for n in range(CAP)],axis=0)
            for mx in range(2):
                pltpu.matmul_push_rhs(cols[:,mx*256:(mx+1)*256],rt%2,mx,transpose=True)
        def issue(q):
            rt,c=divmod(q,8)
            for i4 in range(4):
                i=c*4+i4
                lhs=W[rt*16+s,i:i+1,:]*kt
                for mx in range(2):
                    pltpu.matmul_acc_lhs(accs[mx][q%2][i4],lhs[:,mx*256:(mx+1)*256],load_staged_rhs=(rt%2) if (c==0 and i4==0) else None)
        def post(q):
            rt,c=divmod(q,8)
            xs=[]
            for i4 in range(4):
                i=c*4+i4
                f=(pltpu.matmul_pop(accs[0][q%2][i4])+pltpu.matmul_pop(accs[1][q%2][i4]))*ANG[rt,i:i+1,:]
                f=f.astype(BF)
                xs.append(f[:,:128])
                S1[rt,i]=f[:,128:]
            ys=swap_blocks(lane,xs)
            for n in range(4):
                OUT[buf,dests[rt][1][n],:,c*128:(c+1)*128]=ys[n]
        NQ=RPT*8
        push(0)
        issue(0)
        for q in range(1,NQ):
            if q%8==4 and q//8+1<RPT: push(q//8+1)
            issue(q)
            post(q-1)
        post(NQ-1)
        for rt in range(RPT):
            @pl.when(msm[s,0,rt*8+4]>0)
            def _():
                dd=dests[rt][1]
                def more(c,_):
                    ys=swap_blocks(lane,[S1[rt,c*4+k] for k in range(4)])
                    for n in range(4):
                        OUT[buf,dd[4+n],:,pl.ds(pl.multiple_of(c*128,128),128)]=ys[n]
                    return 0
                lax.fori_loop(0,8,more,0)
        return 0
    def whole(*flat):
        accs=[[flat[0:4],flat[4:8]],[flat[8:12],flat[12:16]]]
        def copy(s,buf):
            return pltpu.make_async_copy(OUT.at[buf,pl.ds(0,8)],out.at[pl.ds(s*8,8)],sem.at[buf])
        def step(s,_):
            buf=lax.rem(s,2)
            @pl.when(s>=2)
            def _(): copy(s-2,buf).wait()
            cnt=jnp.int32(0)
            for rt in range(RPT):
                for n in range(CAP):
                    cnt=cnt+jnp.where(msm[s,0,rt*8+n]>0,1,0)
            for t in range(CAP):
                @pl.when(t>=cnt)
                def _(): OUT[buf,t]=jnp.zeros((D,1024),BF)
            @pl.when(cnt>0)
            def _(): sender(s,accs,None)
            copy(s,buf).start()
            return 0
        lax.fori_loop(0,NS,step,0)
        copy(14,0).wait(); copy(15,1).wait()
    pl.run_scoped(whole,*[pltpu.ACC(mx)((64,256),F32) for mx in range(2) for _ in range(8)])


def gather(wave, kern, labels, rows, cols, owners):
    vm = pl.BlockSpec(memory_space=pltpu.VMEM)
    blocks = jax.ShapeDtypeStruct((2, 4, 4, 4, 16, 128), BF)
    dma = pltpu.SemaphoreType.DMA
    return pl.pallas_call(
        gather_kernel,
        in_specs=[vm] * 6,
        out_specs=[vm] * 5,
        out_shape=[blocks] * 3
        + [jax.ShapeDtypeStruct((NS, 1, 128), jnp.int32), jax.ShapeDtypeStruct((D, 512), BF)],
        scratch_shapes=[
            pltpu.VMEM((NS, 1, 128), jnp.int32),
            dma((3, 3, 3)), dma((3, 3, 3)), dma((NS,)), dma((NS,)), dma((3, 4)), dma((3, 4)),
        ],
        compiler_params=pltpu.CompilerParams(
            collective_id=0, has_side_effects=True, vmem_limit_bytes=24 * 2**20
        ),
    )(wave, kern, labels, rows, cols, owners)


def forms(meta, kt, b0, b1, b2):
    vm = pl.BlockSpec(memory_space=pltpu.VMEM)
    return pl.pallas_call(
        forms_kernel,
        in_specs=[pl.BlockSpec(memory_space=pltpu.SMEM), vm, vm, vm, vm, vm],
        out_specs=pl.BlockSpec(memory_space=pltpu.HBM),
        out_shape=jax.ShapeDtypeStruct((NS * CAP, D, 1024), BF),
        scratch_shapes=[
            pltpu.VMEM((48, 32, 512), BF),
            pltpu.VMEM((2, 9, D, 1024), BF),
            pltpu.VMEM((RPT, 32, D, 128), BF),
            pltpu.VMEM((RPT, 32, 256), F32),
            pltpu.VMEM((RPT, NS, 128), F32),
            pltpu.SemaphoreType.DMA((2,)),
        ],
        compiler_params=pltpu.CompilerParams(vmem_limit_bytes=40 * 2**20),
    )(meta, meta, kt, b0, b1, b2)


def per_device(wavefuncs, kernel, labels, row_tiles, col_tiles, owners):
    label_row = jnp.pad(labels.reshape(1, 96), ((0, 0), (32, 0)))
    b0, b1, b2, meta, kt = gather(
        wavefuncs, kernel, label_row, row_tiles.reshape(1, 64), col_tiles.reshape(1, 64), owners
    )
    return forms(meta, kt, b0, b1, b2)


def solution(mesh):
    return jax.shard_map(
        per_device,
        mesh=mesh,
        in_specs=(P("bin", "dist"), P(None, "dist"), P("bin"), P("bin"), P("bin"), P("bin", None)),
        out_specs=P("bin", "dist", None),
        check_vma=False,
    )
```

```python
import functools
import jax
import jax.numpy as jnp
from jax import lax
from jax.experimental import pallas as pl
from jax.experimental.pallas import tpu as pltpu
from jax.sharding import PartitionSpec as P

D = 64
RPT = 3
CAP = 8
NS = 16
BF = jnp.bfloat16
F32 = jnp.float32
MESH = pl.DeviceIdType.MESH


def gather_kernel(wave_in, labels_in, rows_in, cols_in, owners_in, b0, b1, b2, meta,
                  table, wave, labels, rows, cols, owners, in_sem,
                  z_send, z_recv, m_send, m_recv, c_send, c_recv):
    loads = [
        pltpu.make_async_copy(src, dst, in_sem.at[k])
        for k, (src, dst) in enumerate(
            ((wave_in, wave), (labels_in, labels), (rows_in, rows), (cols_in, cols), (owners_in, owners))
        )
    ]
    for load in loads:
        load.start()
    own, own_d = lax.axis_index("bin"), lax.axis_index("dist")
    x, yh, core = own // 4, (own // 2) % 2, own % 2
    z, yl = own_d // 2, own_d % 2
    y = yh * 2 + yl
    other = 1 - core

    def chip(px, py, pz, pc):
        return (px * 4 + (py // 2) * 2 + pc, pz * 2 + py % 2)

    def up(v, o):
        return (v + o) % 4

    barrier = pltpu.get_barrier_semaphore()
    peers = [((own + k) % NS, own_d) for k in range(1, NS)]
    peers += [chip(x, y, up(z, o), core) for o in (1, 2, 3)]
    peers += [chip(x, up(y, o), z, core) for o in (1, 3)]
    for peer in peers:
        pl.semaphore_signal(barrier, inc=1, device_id=peer, device_id_type=MESH)

    for load in loads:
        load.wait()
    shard = wave[...].astype(F32).T
    for rt, b in enumerate((b0, b1, b2)):
        part = jnp.concatenate(
            [shard[rt * 32 : rt * 32 + 16, :], shard[rt * 32 + 16 : rt * 32 + 32, :]], axis=1
        ).astype(BF)
        if rt == 0:
            b[core, x, y, z] = part
        elif rt == 1:
            b[core, z, x, y] = part
        else:
            b[core, y, z, x] = part

    sub64 = lax.broadcasted_iota(jnp.int32, (64, 64), 0)
    lan64 = lax.broadcasted_iota(jnp.int32, (64, 64), 1)

    def column(row):
        return jnp.sum(jnp.where(sub64 == lan64, jnp.broadcast_to(row, (64, 64)), 0), axis=1, keepdims=True)

    own_r, col_r = owners[...], cols[...]
    own_c = column(own_r)
    same = (jnp.broadcast_to(own_c, (64, 64)) == own_r) & (lan64 < sub64)
    slot_c = jnp.sum(jnp.where(same, 1, 0), axis=1, keepdims=True)
    third = lax.shift_right_logical(col_r * 171, 9)
    code_c = column(1 + rows[...] * 64 + (col_r - 3 * third) * 16 + third)
    lane64 = lax.broadcasted_iota(jnp.int32, (64, 128), 1)
    lane1 = lax.broadcasted_iota(jnp.int32, (1, 128), 1)
    spread = jnp.where(lane64 == slot_c, jnp.broadcast_to(code_c, (64, 128)), 0)
    label_row = jnp.concatenate([jnp.zeros((1, 32), jnp.int32), labels[...]], axis=1)
    for o in range(NS):
        mine = jnp.where(own_c == o, spread, 0)
        table[o] = jnp.where(lane1 < 32, jnp.sum(mine, axis=0, keepdims=True), label_row)

    meta[own] = table[own]

    pl.semaphore_wait(barrier, len(peers))

    def copy(src, dst, send, recv, device):
        return pltpu.make_async_remote_copy(
            src_ref=src, dst_ref=dst, send_sem=send, recv_sem=recv, device_id=device, device_id_type=MESH
        )

    sent = []

    def block(rt, stage, v, c):
        if rt == 0:
            return (b0.at[c, x, y, v], b0.at[c, x, v], b0.at[c, v])[stage]
        if rt == 1:
            return (b1.at[c, z, x, v], b1.at[c, z, v], b1.at[c, v])[stage]
        return (b2.at[c, y, z, v], b2.at[c, y, v], b2.at[c, v])[stage]

    def place(rt, stage):
        axis = ("zyx", "yxz", "xzy")[rt][stage]
        return {"x": x, "y": y, "z": z}[axis], axis

    def device(axis, v):
        return chip(v if axis == "x" else x, v if axis == "y" else y, v if axis == "z" else z, core)

    def push(rt, stage):
        at, axis = place(rt, stage)
        for o in (1, 3, 2):
            cp = copy(block(rt, stage, at, core), block(rt, stage, at, core),
                      z_send.at[rt, stage, o - 1], z_recv.at[rt, stage, o - 1], device(axis, up(at, o)))
            cp.start()
            sent.append(cp)

    def landed(rt, stage, o):
        at, axis = place(rt, stage)
        v = up(at, 4 - o)
        copy(block(rt, stage, v, core), block(rt, stage, v, core),
             z_send.at[rt, stage, o - 1], z_recv.at[rt, stage, o - 1], device(axis, v)).wait_recv()
        return v

    def across(rt, k, v, c):
        return copy(block(rt, 2, v, c), block(rt, 2, v, c), c_send.at[rt, k], c_recv.at[rt, k], chip(x, y, z, other))

    for rt in range(RPT):
        push(rt, 0)
    for k in range(1, NS):
        to = (own + k) % NS
        cp = copy(table.at[to], meta.at[own], m_send.at[k], m_recv.at[k], (to, own_d))
        cp.start()
        sent.append(cp)
    for rt in range(RPT):
        for o in (1, 3, 2):
            landed(rt, 0, o)
        push(rt, 1)
    for rt in range(RPT):
        for o in (1, 3, 2):
            landed(rt, 1, o)
        push(rt, 2)
        cp = across(rt, 0, place(rt, 2)[0], core)
        cp.start()
        sent.append(cp)
    for o in (1, 3, 2):
        for rt in range(RPT):
            v = landed(rt, 2, o)
            cp = across(rt, o, v, core)
            cp.start()
            sent.append(cp)
    for k in range(1, NS):
        at = (own + NS - k) % NS
        copy(table.at[at], meta.at[at], m_send.at[k], m_recv.at[k], (at, own_d)).wait_recv()
    for o in (0, 1, 3, 2):
        for rt in range(RPT):
            across(rt, o, up(place(rt, 2)[0], (4 - o) % 4), other).wait_recv()
    for cp in sent:
        cp.wait_send()


def swap_blocks(lane, x):
    half=lane<64
    even=(lane//32)%2==0
    def cross(p,q,shift,mask):
        return jnp.where(mask,p,pltpu.roll(q,shift,1)), jnp.where(mask,pltpu.roll(p,128-shift,1),q)
    a0,a2=cross(x[0],x[2],64,half)
    a1,a3=cross(x[1],x[3],64,half)
    y0,y1=cross(a0,a1,32,even)
    y2,y3=cross(a2,a3,32,even)
    return y0,y1,y2,y3

def forms_kernel(msm, mv, kt_in, b0, b1, b2, out, W, OUT, ANG, LT, LC, kt_ref, sem):
    load=pltpu.make_async_copy(kt_in,kt_ref,sem.at[2])
    load.start()
    lane16=lax.broadcasted_iota(jnp.int32,(16,128),1)
    lane=lax.broadcasted_iota(jnp.int32,(64,128),1)
    lo=lane16<64
    for rt,b in enumerate((b0,b1,b2)):
        for x in range(4):
            for yh in range(2):
                for c in range(2):
                    s=x*4+yh*2+c
                    for z in range(4):
                        def at(yl):
                            y=yh*2+yl
                            return b[c,x,y,z] if rt==0 else (b[c,z,x,y] if rt==1 else b[c,y,z,x])
                        p,q=at(0),at(1)
                        W[rt*16+s,0:16,z*128:(z+1)*128]=jnp.concatenate([p[:,:64],q[:,:64]],axis=1)
                        W[rt*16+s,16:32,z*128:(z+1)*128]=jnp.concatenate([p[:,64:],q[:,64:]],axis=1)
    m=mv[...].astype(F32).reshape(16,128)
    rolls=[m]+[pltpu.roll(m,32*k,1) for k in (1,2,3)]
    for rt in range(RPT):
        acc=rolls[(0-rt-1)%4]
        for g in (1,2,3):
            acc=jnp.where(lane16//32==g,rolls[(g-rt-1)%4],acc)
        LT[rt]=acc

    W[48]=jnp.zeros((32,512),BF)
    eye=(lax.broadcasted_iota(jnp.int32,(32,128),1)==lax.broadcasted_iota(jnp.int32,(32,128),0))
    blk=lax.broadcasted_iota(jnp.int32,(32,128),1)//32
    load.wait()
    kt=kt_ref[...]
    I8=8

    def codes(s):
        out=[]
        for n in range(CAP):
            code=msm[s,0,n]
            cm=jnp.maximum(code-1,0)
            out.append((code>0,cm>>6,cm&63))
        return out

    def prep(s):
        cs=codes(s)
        for rt in range(RPT):
            lrow=LT[rt,pl.ds(s,1),:]
            li=jnp.sum(jnp.where(eye,jnp.broadcast_to(lrow,(32,128)),0.0),axis=1,keepdims=True)
            LC[rt]=jnp.broadcast_to(li,(32,128))
        for h in range(2):
            lj=li=None
            for g in range(4):
                _,rt,t=cs[h*4+g]
                row=jnp.broadcast_to(LT[t>>4,pl.ds(t&15,1),:],(32,128))
                col=LC[rt]
                lj=row if lj is None else jnp.where(blk==g,row,lj)
                li=col if li is None else jnp.where(blk==g,col,li)
            ANG[lax.rem(s,2),:,h*128:(h+1)*128]=jnp.sqrt((2.0*li+1.0)*(2.0*lj+1.0))/(8.0*(1.0+jnp.abs(li-lj)))

    def push(s,k):
        rt=k%3
        tiles=[W[jnp.where(ok&(r==rt),t,48)] for ok,r,t in codes(s)]
        cols=jnp.concatenate(tiles,axis=0)
        for mx in range(2):
            pltpu.matmul_push_rhs(cols[:,mx*256:(mx+1)*256],k%2,mx,transpose=True)

    def issue(accs,s,k,snext,knext):
        c,rt=divmod(k,3)
        for i8 in range(I8):
            i=c*I8+i8
            lhs=W[rt*16+s,i:i+1,:]*kt
            for mx in range(2):
                pltpu.matmul_acc_lhs(accs[mx][c%2][i8],lhs[:,mx*256:(mx+1)*256],load_staged_rhs=(k%2) if i8==0 else None)
            if i8==0: push(snext,knext)

    def post(accs,s,c,half):
        buf=lax.rem(s,2)
        lows,highs=[],[]
        for i4 in range(4):
            i8=half*4+i4
            i=c*I8+i8
            f=(pltpu.matmul_pop(accs[0][c%2][i8])+pltpu.matmul_pop(accs[1][c%2][i8]))*ANG[buf,i:i+1,:]
            f=f.astype(BF)
            lows.append(f[:,:128]); highs.append(f[:,128:])
        q=c*2+half
        for base,xs in ((0,lows),(4,highs)):
            for n,v in enumerate(swap_blocks(lane,xs)):
                OUT[buf,base+n,:,q*128:(q+1)*128]=v

    def whole(*flat):
        accs=[[flat[mx*16+b*8:mx*16+b*8+8] for b in range(2)] for mx in range(2)]
        def copy(s,buf):
            return pltpu.make_async_copy(OUT.at[buf],out.at[pl.ds(s*8,8)],sem.at[buf])
        prep(0)
        push(0,0)
        issue(accs,0,0,0,1)
        def step(s,_):
            buf=lax.rem(s,2)
            nxt=jnp.minimum(s+1,NS-1)
            @pl.when(s>=2)
            def _(): copy(s-2,buf).wait()
            for k in range(1,13):
                if k<12:
                    issue(accs,s,k,s if k<11 else nxt,(k+1)%12)
                else:
                    issue(accs,nxt,0,nxt,1)
                c,rt=divmod(k,3)
                if c>0 and rt<2 and k<12: post(accs,s,c-1,rt)
                if k==6: prep(nxt)
            post(accs,s,3,0)
            post(accs,s,3,1)
            copy(s,buf).start()
            return 0
        lax.fori_loop(0,NS,step,0)
        for mx in range(2):
            pltpu.matmul_acc_lhs(accs[mx][0][0],kt[:,mx*256:(mx+1)*256],load_staged_rhs=1)
        tot=jnp.zeros((64,256),F32)
        for mx in range(2):
            for i8 in range(I8):
                tot=tot+pltpu.matmul_pop(accs[mx][0][i8])
        ANG[0]=tot[0:32]
        copy(14,0).wait(); copy(15,1).wait()
    pl.run_scoped(whole,*[pltpu.ACC(mx)((64,256),F32) for mx in range(2) for _ in range(16)])


def gather(wave, labels, rows, cols, owners):
    vm = pl.BlockSpec(memory_space=pltpu.VMEM)
    blocks = jax.ShapeDtypeStruct((2, 4, 4, 4, 16, 128), BF)
    dma = pltpu.SemaphoreType.DMA
    return pl.pallas_call(
        gather_kernel,
        in_specs=[pl.BlockSpec(memory_space=pltpu.HBM)] * 5,
        out_specs=[vm] * 4,
        out_shape=[blocks] * 3 + [jax.ShapeDtypeStruct((NS, 1, 128), jnp.int32)],
        scratch_shapes=[
            pltpu.VMEM((NS, 1, 128), jnp.int32),
            pltpu.VMEM((64, 96), BF),
            pltpu.VMEM((1, 96), jnp.int32),
            pltpu.VMEM((1, 64), jnp.int32),
            pltpu.VMEM((1, 64), jnp.int32),
            pltpu.VMEM((1, 64), jnp.int32),
            dma((5,)),
            dma((3, 3, 3)), dma((3, 3, 3)), dma((NS,)), dma((NS,)), dma((3, 4)), dma((3, 4)),
        ],
        compiler_params=pltpu.CompilerParams(
            collective_id=0, has_side_effects=True, vmem_limit_bytes=24 * 2**20
        ),
    )(wave, labels, rows, cols, owners)


def forms(meta, kt, b0, b1, b2):
    vm = pl.BlockSpec(memory_space=pltpu.VMEM)
    return pl.pallas_call(
        forms_kernel,
        in_specs=[pl.BlockSpec(memory_space=pltpu.SMEM), vm, pl.BlockSpec(memory_space=pltpu.HBM), vm, vm, vm],
        out_specs=pl.BlockSpec(memory_space=pltpu.HBM),
        out_shape=jax.ShapeDtypeStruct((NS * CAP, D, 1024), BF),
        scratch_shapes=[
            pltpu.VMEM((49, 32, 512), BF),
            pltpu.VMEM((2, CAP, D, 1024), BF),
            pltpu.VMEM((2, 32, 256), F32),
            pltpu.VMEM((RPT, NS, 128), F32),
            pltpu.VMEM((RPT, 32, 128), F32),
            pltpu.VMEM((D, 512), BF),
            pltpu.SemaphoreType.DMA((3,)),
        ],
        compiler_params=pltpu.CompilerParams(vmem_limit_bytes=40 * 2**20),
    )(meta, meta, kt, b0, b1, b2)


def per_device(wavefuncs, kernel, labels, row_tiles, col_tiles, owners):
    def in_hbm(v):
        return pltpu.with_memory_space_constraint(v, pltpu.HBM)

    b0, b1, b2, meta = gather(
        in_hbm(wavefuncs.T),
        in_hbm(labels.reshape(1, 96)),
        in_hbm(row_tiles.reshape(1, 64)),
        in_hbm(col_tiles.reshape(1, 64)),
        in_hbm(owners.T),
    )
    return forms(meta, in_hbm(kernel.T), b0, b1, b2)


def solution(mesh):
    return jax.shard_map(
        per_device,
        mesh=mesh,
        in_specs=(P("bin", "dist"), P(None, "dist"), P("bin"), P("bin"), P("bin"), P("bin", None)),
        out_specs=P("bin", "dist", None),
        check_vma=False,
    )
```

```python
import functools
import jax
import jax.numpy as jnp
from jax import lax
from jax.experimental import pallas as pl
from jax.experimental.pallas import tpu as pltpu
from jax.sharding import PartitionSpec as P

D = 64
RPT = 3
CAP = 8
NS = 16
BF = jnp.bfloat16
F32 = jnp.float32
MESH = pl.DeviceIdType.MESH


def gather_kernel(wave_in, labels_in, rows_in, cols_in, owners_in, kt_in, w_all, lt, meta, kt,
                  b0, b1, b2, table, via_x, via_y, wave, labels, rows, cols, owners, in_sem,
                  z_send, z_recv, c_send, c_recv, m_send, m_recv):
    loads = [
        pltpu.make_async_copy(src, dst, in_sem.at[k])
        for k, (src, dst) in enumerate(
            ((wave_in, wave), (labels_in, labels), (rows_in, rows), (cols_in, cols), (owners_in, owners), (kt_in, kt))
        )
    ]
    for load in loads:
        load.start()
    own, own_d = lax.axis_index("bin"), lax.axis_index("dist")
    x, yh, core = own // 4, (own // 2) % 2, own % 2
    z, yl = own_d // 2, own_d % 2
    y = yh * 2 + yl
    other = 1 - core

    def chip(px, py, pz, pc):
        return (px * 4 + (py // 2) * 2 + pc, pz * 2 + py % 2)

    def up(v, o):
        return (v + o) % 4

    def peer(axis, o):
        return chip(
            up(x, o) if axis == "x" else x, up(y, o) if axis == "y" else y, up(z, o) if axis == "z" else z, core
        )

    barrier = pltpu.get_barrier_semaphore()
    peers = [peer(axis, o) for o in (2, 1, 3) for axis in "xyz"] + [chip(x, y, z, other)]
    for at in peers:
        pl.semaphore_signal(barrier, inc=1, device_id=at, device_id_type=MESH)

    loads[0].wait()
    shard = wave[...].astype(F32).T
    for rt, b in enumerate((b0, b1, b2)):
        part = jnp.concatenate(
            [shard[rt * 32 : rt * 32 + 16, :], shard[rt * 32 + 16 : rt * 32 + 32, :]], axis=1
        ).astype(BF)
        if rt == 0:
            b[core, x, y, z] = part
        elif rt == 1:
            b[core, z, x, y] = part
        else:
            b[core, y, z, x] = part

    pl.semaphore_wait(barrier, len(peers))

    def copy(src, dst, send, recv, device):
        return pltpu.make_async_remote_copy(
            src_ref=src, dst_ref=dst, send_sem=send, recv_sem=recv, device_id=device, device_id_type=MESH
        )

    def taken(ref, send):
        copy(ref, ref, send, send, peers[0]).wait_send()

    def arrived(ref, recv):
        copy(ref, ref, recv, recv, peers[0]).wait_recv()

    def block(rt, stage, v, c):
        if rt == 0:
            return (b0.at[c, x, y, v], b0.at[c, x, v], b0.at[c, v])[stage]
        if rt == 1:
            return (b1.at[c, z, x, v], b1.at[c, z, v], b1.at[c, v])[stage]
        return (b2.at[c, y, z, v], b2.at[c, y, v], b2.at[c, v])[stage]

    def place(rt, stage):
        axis = ("zyx", "yxz", "xzy")[rt][stage]
        return {"x": x, "y": y, "z": z}[axis], axis

    def push(rt, stage):
        at, axis = place(rt, stage)
        mine = block(rt, stage, at, core)
        for o in (2, 1, 3):
            recv = z_recv.at[rt, stage + (stage == 2 and o == 2)]
            copy(mine, mine, z_send.at[rt, stage], recv, peer(axis, o)).start()

    def some(rt, stage, n):
        b = (b0, b1, b2)[rt]
        return (b.at[0, 0, 0, pl.ds(0, n)], b.at[0, 0, pl.ds(0, n)], b.at[0, pl.ds(0, n)])[stage]

    def across(rt, o, k):
        v = up(place(rt, 2)[0], (4 - o) % 4)
        copy(block(rt, 2, v, core), block(rt, 2, v, core), c_send.at[rt], c_recv.at[rt, k], chip(x, y, z, other)).start()

    def lay_stage(rt, c, o):
        if rt < 2:
            lay_plane(rt, up(place(rt, 2)[0], (4 - o) % 4), c)

    def lay(rt, c, px, h, pz, even, odd):
        tile = rt * 16 + c * 8 + h * 4 + px
        lanes = pl.ds(pl.multiple_of(pz * 128, 128), 128)
        w_all[tile, 0:16, lanes] = jnp.concatenate([even[:, :64], odd[:, :64]], axis=1)
        w_all[tile, 16:32, lanes] = jnp.concatenate([even[:, 64:], odd[:, 64:]], axis=1)

    def lay_plane(rt, v, c):
        if rt == 0:
            for h in range(2):
                for pz in range(4):
                    lay(0, c, v, h, pz, b0[c, v, 2 * h, pz], b0[c, v, 2 * h + 1, pz])
        elif rt == 1:
            for px in range(4):
                for h in range(2):
                    lay(1, c, px, h, v, b1[c, v, px, 2 * h], b1[c, v, px, 2 * h + 1])
        else:
            for pz in range(4):
                for px in range(4):
                    lay(2, c, px, v, pz, b2[c, 2 * v, pz, px], b2[c, 2 * v + 1, pz, px])

    for rt in range(RPT):
        push(rt, 0)

    for load in loads[1:]:
        load.wait()
    sub64 = lax.broadcasted_iota(jnp.int32, (64, 64), 0)
    lan64 = lax.broadcasted_iota(jnp.int32, (64, 64), 1)

    def column(row):
        return jnp.sum(jnp.where(sub64 == lan64, jnp.broadcast_to(row, (64, 64)), 0), axis=1, keepdims=True)

    own_r, col_r = owners[...], cols[...]
    own_c = column(own_r)
    same = (jnp.broadcast_to(own_c, (64, 64)) == own_r) & (lan64 < sub64)
    slot_c = jnp.sum(jnp.where(same, 1, 0), axis=1, keepdims=True)
    third = lax.shift_right_logical(col_r * 171, 9)
    number = (third & 1) * 8 + (third & 2) * 2 + lax.shift_right_logical(third, 2)
    code_c = column(1 + rows[...] * 64 + (col_r - 3 * third) * 16 + number)
    lane64 = lax.broadcasted_iota(jnp.int32, (64, 128), 1)
    lane1 = lax.broadcasted_iota(jnp.int32, (1, 128), 1)
    spread = jnp.where(lane64 == slot_c, jnp.broadcast_to(code_c, (64, 128)), 0)
    label_row = jnp.concatenate([jnp.zeros((1, 32), jnp.int32), labels[...]], axis=1)
    for o in range(NS):
        mine = jnp.where(own_c == o, spread, 0)
        table[o // 4, o % 4] = jnp.where(lane1 < 32, jnp.sum(mine, axis=0, keepdims=True), label_row)

    for o in (2, 1, 3):
        copy(table.at[up(x, o)], via_x.at[x], m_send.at[0], m_recv.at[0], peer("x", o)).start()
    via_x[x] = table[x]

    for rt in range(RPT):
        arrived(some(rt, 0, 3), z_recv.at[rt, 0])
        push(rt, 1)
    for rt in range(RPT):
        taken(some(rt, 0, 3), z_send.at[rt, 0])

    arrived(via_x.at[pl.ds(0, 3)], m_recv.at[0])
    taken(table.at[pl.ds(0, 3)], m_send.at[0])
    far = 1 - yh
    meta_y = copy(via_x.at[:, pl.ds(far * 2, 2)], via_y.at[yh], m_send.at[1], m_recv.at[1], peer("y", 2))
    meta_y.start()
    via_y[yh] = via_x[:, pl.ds(yh * 2, 2)]

    for rt in range(RPT):
        arrived(some(rt, 1, 3), z_recv.at[rt, 1])
        push(rt, 2)
        across(rt, 0, 0)
    for rt in range(RPT):
        taken(some(rt, 1, 3), z_send.at[rt, 1])

    arrived(via_y.at[far], m_recv.at[1])
    meta_c = copy(via_y.at[:, :, other], meta.at[core], m_send.at[2], m_recv.at[2], chip(x, y, z, other))
    meta_c.start()
    meta_y.wait_send()
    meta[core] = via_y[:, :, core]
    w_all[48] = jnp.zeros((32, 512), BF)
    lay_plane(0, x, core)
    lay_plane(1, z, core)

    arrived(meta.at[other], m_recv.at[2])
    meta_c.wait_send()
    lane16 = lax.broadcasted_iota(jnp.int32, (NS, 128), 1)
    found = jnp.concatenate([meta[c, h, p] for c in range(2) for h in range(2) for p in range(4)], axis=0)
    found = found.astype(F32)
    rolled = [found] + [pltpu.roll(found, 32 * k, 1) for k in (1, 2, 3)]
    for rt in range(RPT):
        labs = rolled[(0 - rt - 1) % 4]
        for g in (1, 2, 3):
            labs = jnp.where(lane16 // 32 == g, rolled[(g - rt - 1) % 4], labs)
        lt[rt] = labs
    for rt in range(RPT):
        arrived(some(rt, 2, 2), z_recv.at[rt, 2])
        across(rt, 1, 1)
        across(rt, 3, 1)
    for rt in range(RPT):
        arrived(some(rt, 2, 1), c_recv.at[rt, 0])
        lay_stage(rt, other, 0)
        lay_stage(rt, core, 1)
        lay_stage(rt, core, 3)
    lay_plane(2, yh, core)
    for rt in range(RPT):
        arrived(some(rt, 2, 1), z_recv.at[rt, 3])
        across(rt, 2, 2)
    for rt in range(RPT):
        arrived(some(rt, 2, 2), c_recv.at[rt, 1])
        lay_stage(rt, other, 1)
        lay_stage(rt, other, 3)
        lay_stage(rt, core, 2)
    lay_plane(2, yh, other)
    lay_plane(2, far, core)
    for rt in range(RPT):
        taken(some(rt, 2, 3), z_send.at[rt, 2])
    for rt in range(RPT):
        arrived(some(rt, 2, 1), c_recv.at[rt, 2])
        lay_stage(rt, other, 2)
    lay_plane(2, far, other)
    for rt in range(RPT):
        taken(some(rt, 2, 4), c_send.at[rt])


def swap_blocks(lane, x):
    half=lane<64
    even=(lane//32)%2==0
    def cross(p,q,shift,mask):
        return jnp.where(mask,p,pltpu.roll(q,shift,1)), jnp.where(mask,pltpu.roll(p,128-shift,1),q)
    a0,a2=cross(x[0],x[2],64,half)
    a1,a3=cross(x[1],x[3],64,half)
    y0,y1=cross(a0,a1,32,even)
    y2,y3=cross(a2,a3,32,even)
    return y0,y1,y2,y3

def forms_kernel(msm, W, LT, kt_ref, out, OUT, ANG, LC, sem):
    lane=lax.broadcasted_iota(jnp.int32,(64,128),1)
    eye=(lax.broadcasted_iota(jnp.int32,(32,128),1)==lax.broadcasted_iota(jnp.int32,(32,128),0))
    blk=lax.broadcasted_iota(jnp.int32,(32,128),1)//32
    kt=kt_ref[...]
    I8=8

    def codes(s):
        out=[]
        for n in range(CAP):
            code=msm[s,0,n]
            cm=jnp.maximum(code-1,0)
            out.append((code>0,cm>>6,cm&63))
        return out

    def prep(s):
        cs=codes(s)
        for rt in range(RPT):
            lrow=LT[rt,pl.ds(s,1),:]
            li=jnp.sum(jnp.where(eye,jnp.broadcast_to(lrow,(32,128)),0.0),axis=1,keepdims=True)
            LC[rt]=jnp.broadcast_to(li,(32,128))
        for h in range(2):
            lj=li=None
            for g in range(4):
                _,rt,t=cs[h*4+g]
                row=jnp.broadcast_to(LT[t>>4,pl.ds(t&15,1),:],(32,128))
                col=LC[rt]
                lj=row if lj is None else jnp.where(blk==g,row,lj)
                li=col if li is None else jnp.where(blk==g,col,li)
            ANG[lax.rem(s,2),:,h*128:(h+1)*128]=jnp.sqrt((2.0*li+1.0)*(2.0*lj+1.0))/(8.0*(1.0+jnp.abs(li-lj)))

    def rt_of(k):
        c,p=divmod(k%12,3)
        return p if c%2==0 else 2-p
    fresh=[k for k in range(12) if k==0 or rt_of(k)!=rt_of(k-1)]
    def push(s,k):
        rt=rt_of(k)
        tiles=[W[jnp.where(ok&(r==rt),t,48)] for ok,r,t in codes(s)]
        cols=jnp.concatenate(tiles,axis=0)
        for mx in range(2):
            pltpu.matmul_push_rhs(cols[:,mx*256:(mx+1)*256],fresh.index(k)%2,mx,transpose=True)

    def issue(accs,s,k,snext):
        c=k//3
        rt=rt_of(k)
        for i8 in range(I8):
            i=c*I8+i8
            lhs=W[rt*16+s,i:i+1,:]*kt
            for mx in range(2):
                pltpu.matmul_acc_lhs(accs[mx][c%2][i8],lhs[:,mx*256:(mx+1)*256],load_staged_rhs=(fresh.index(k)%2) if i8==0 and k in fresh else None)
            if i8==0 and k in fresh:
                j=fresh.index(k)+1
                push(s if j<len(fresh) else snext,fresh[j%len(fresh)])

    def post(accs,s,c,half):
        buf=lax.rem(s,2)
        lows,highs=[],[]
        for i4 in range(4):
            i8=half*4+i4
            i=c*I8+i8
            f=(pltpu.matmul_pop(accs[0][c%2][i8])+pltpu.matmul_pop(accs[1][c%2][i8]))*ANG[buf,i:i+1,:]
            f=f.astype(BF)
            lows.append(f[:,:128]); highs.append(f[:,128:])
        q=c*2+half
        for base,xs in ((0,lows),(4,highs)):
            for n,v in enumerate(swap_blocks(lane,xs)):
                OUT[buf,base+n,:,q*128:(q+1)*128]=v

    def whole(*flat):
        accs=[[flat[mx*16+b*8:mx*16+b*8+8] for b in range(2)] for mx in range(2)]
        def copy(s,buf):
            place=(s%4)*4+((s//4)%2)*2+s//8
            return pltpu.make_async_copy(OUT.at[buf],out.at[pl.ds(place*8,8)],sem.at[buf])
        prep(0)
        push(0,0)
        issue(accs,0,0,0)
        def step(s,_):
            buf=lax.rem(s,2)
            nxt=jnp.minimum(s+1,NS-1)
            @pl.when(s>=2)
            def _(): copy(s-2,buf).wait()
            for k in range(1,13):
                if k<12:
                    issue(accs,s,k,nxt)
                else:
                    issue(accs,nxt,0,nxt)
                c,p=divmod(k,3)
                if c>0 and p<2 and k<12: post(accs,s,c-1,p)
                if k==6: prep(nxt)
            post(accs,s,3,0)
            post(accs,s,3,1)
            copy(s,buf).start()
            return 0
        lax.fori_loop(0,NS,step,0)
        for mx in range(2):
            pltpu.matmul_acc_lhs(accs[mx][0][0],kt[:,mx*256:(mx+1)*256],load_staged_rhs=1)
        tot=jnp.zeros((64,256),F32)
        for mx in range(2):
            for i8 in range(I8):
                tot=tot+pltpu.matmul_pop(accs[mx][0][i8])
        ANG[0]=tot[0:32]
        copy(14,0).wait(); copy(15,1).wait()
    pl.run_scoped(whole,*[pltpu.ACC(mx)((64,256),F32) for mx in range(2) for _ in range(16)])

def gather(wave, labels, rows, cols, owners, kt):
    vm = pl.BlockSpec(memory_space=pltpu.VMEM)
    blocks = pltpu.VMEM((2, 4, 4, 4, 16, 128), BF)
    i32 = jnp.int32
    dma = pltpu.SemaphoreType.DMA
    return pl.pallas_call(
        gather_kernel,
        in_specs=[pl.BlockSpec(memory_space=pltpu.HBM)] * 6,
        out_specs=[vm] * 4,
        out_shape=[
            jax.ShapeDtypeStruct((49, 32, 512), BF),
            jax.ShapeDtypeStruct((RPT, NS, 128), F32),
            jax.ShapeDtypeStruct((2, 2, 4, 1, 128), i32),
            jax.ShapeDtypeStruct((D, 512), BF),
        ],
        scratch_shapes=[
            blocks, blocks, blocks,
            pltpu.VMEM((4, 4, 1, 128), i32),
            pltpu.VMEM((4, 4, 1, 128), i32),
            pltpu.VMEM((2, 4, 2, 1, 128), i32),
            pltpu.VMEM((64, 96), BF),
            pltpu.VMEM((1, 96), i32),
            pltpu.VMEM((1, 64), i32),
            pltpu.VMEM((1, 64), i32),
            pltpu.VMEM((1, 64), i32),
            dma((6,)),
            dma((3, 3)), dma((3, 4)), dma((3,)), dma((3, 3)), dma((3,)), dma((3,)),
        ],
        compiler_params=pltpu.CompilerParams(
            collective_id=0, has_side_effects=True, vmem_limit_bytes=24 * 2**20
        ),
    )(wave, labels, rows, cols, owners, kt)


def forms(meta, w_all, lt, kt):
    vm = pl.BlockSpec(memory_space=pltpu.VMEM)
    return pl.pallas_call(
        forms_kernel,
        in_specs=[pl.BlockSpec(memory_space=pltpu.SMEM), vm, vm, vm],
        out_specs=pl.BlockSpec(memory_space=pltpu.HBM),
        out_shape=jax.ShapeDtypeStruct((NS * CAP, D, 1024), BF),
        scratch_shapes=[
            pltpu.VMEM((2, CAP, D, 1024), BF),
            pltpu.VMEM((2, 32, 256), F32),
            pltpu.VMEM((RPT, 32, 128), F32),
            pltpu.SemaphoreType.DMA((2,)),
        ],
        compiler_params=pltpu.CompilerParams(vmem_limit_bytes=40 * 2**20),
    )(meta, w_all, lt, kt)


def per_device(wavefuncs, kernel, labels, row_tiles, col_tiles, owners):
    def in_hbm(v):
        return pltpu.with_memory_space_constraint(v, pltpu.HBM)

    w_all, lt, meta, kt = gather(
        in_hbm(wavefuncs.T),
        in_hbm(labels.reshape(1, 96)),
        in_hbm(row_tiles.reshape(1, 64)),
        in_hbm(col_tiles.reshape(1, 64)),
        in_hbm(owners.T),
        in_hbm(kernel.T),
    )
    return forms(meta.reshape(NS, 1, 128), w_all, lt, kt)


def solution(mesh):
    return jax.shard_map(
        per_device,
        mesh=mesh,
        in_specs=(P("bin", "dist"), P(None, "dist"), P("bin"), P("bin"), P("bin"), P("bin", None)),
        out_specs=P("bin", "dist", None),
        check_vma=False,
    )
```

```python
import functools
import jax
import jax.numpy as jnp
from jax import lax
from jax.experimental import pallas as pl
from jax.experimental.pallas import tpu as pltpu
from jax.sharding import PartitionSpec as P

D = 64
RPT = 3
CAP = 8
NS = 16
BF = jnp.bfloat16
F32 = jnp.float32
MESH = pl.DeviceIdType.MESH


TILES, DEST, ROW, PAIR, PAIR_TILE = 0, 16, 24, 27, 29


def factor(li, lj):
    return jnp.sqrt((2.0 * li + 1.0) * (2.0 * lj + 1.0)) / (8.0 * (1.0 + jnp.abs(li - lj)))


def tables(meta, roles, ang, ang_pair):
    lane = lax.broadcasted_iota(jnp.int32, (NS, 128), 1)
    sender = lax.broadcasted_iota(jnp.int32, (NS, 128), 0)
    found = jnp.concatenate([meta[c, h, p] for c in range(2) for h in range(2) for p in range(4)], axis=0)
    ok = (found > 0) & (lane < CAP)
    at = jnp.maximum(found - 1, 0)
    row, tile = at >> 6, at & 63

    def total(mask, value):
        return jnp.sum(jnp.where(mask, value, 0), axis=1, keepdims=True)

    n = [total(ok & (row == r), 1) for r in range(RPT)]
    third = jnp.where((n[0] <= n[1]) & (n[0] <= n[2]), 0, jnp.where(n[1] <= n[2], 1, 2))
    first = jnp.where(third == 0, 1, 0)
    second = jnp.where(third == 2, 1, 2)
    single = ok & (row == third)
    p0 = jnp.min(jnp.where(single, lane, CAP), axis=1, keepdims=True)
    p1 = jnp.max(jnp.where(single, lane, -1), axis=1, keepdims=True)
    p1 = jnp.where((p1 == p0) | (p1 < 0), CAP, p1)
    t0 = jnp.where(p0 < CAP, total(single & (lane == p0), tile), 48)
    t1 = jnp.where(p1 < CAP, total(single & (lane == p1), tile), 48)
    role = jnp.where(ok & (row == first), tile, 48)
    role = jnp.where(lane < 8, role, pltpu.roll(jnp.where(ok & (row == second), tile, 48), 8, 1))
    role = jnp.where(lane < 16, role, pltpu.roll(jnp.where(single, CAP, lane), 16, 1))
    for k, v in enumerate((first * 16 + sender, second * 16 + sender, third * 16 + sender, p0, p1, t0, t1)):
        role = jnp.where(lane == ROW + k, v, role)
    for s in range(NS):
        roles[s] = role[s : s + 1, :]

    real = found.astype(F32)
    rolled = [real] + [pltpu.roll(real, 32 * k, 1) for k in (1, 2, 3)]
    labels = []
    for rt in range(RPT):
        v = rolled[(0 - rt - 1) % 4]
        for g in (1, 2, 3):
            v = jnp.where(lane // 32 == g, rolled[(g - rt - 1) % 4], v)
        labels.append(v)
    row_of = [jnp.take_along_axis(row, lane // 32 + 4 * h, axis=1) for h in range(2)]
    tile_of = [jnp.take_along_axis(tile, lane // 32 + 4 * h, axis=1) for h in range(2)]
    tile_of += [jnp.broadcast_to(t, (NS, 128)) for t in (t0, t1)]
    col = [jnp.zeros((NS, 128), F32) for _ in tile_of]
    for t in range(48):
        of = jnp.broadcast_to(labels[t // 16][t % 16 : t % 16 + 1, :], (NS, 128))
        col = [jnp.where(which == t, of, v) for which, v in zip(tile_of, col)]
    of_third = jnp.where(third == 0, labels[0], jnp.where(third == 1, labels[1], labels[2]))
    lane32 = lax.broadcasted_iota(jnp.int32, (32, 128), 1)
    eye = lane32 == lax.broadcasted_iota(jnp.int32, (32, 128), 0)
    spread = lax.broadcasted_iota(jnp.int32, (8, 128), 0) * 4 + lax.broadcasted_iota(jnp.int32, (8, 128), 1) // 32

    def line(v, s, rows):
        return jnp.broadcast_to(v[s : s + 1, :], (rows, 128))

    for s in range(NS):
        down = [jnp.sum(jnp.where(eye, line(labels[rt], s, 32), 0.0), axis=1, keepdims=True) for rt in range(RPT)]
        for h in range(2):
            r = line(row_of[h], s, 32)
            li = jnp.where(r == 0, down[0], jnp.where(r == 1, down[1], down[2]))
            ang[s, :, h * 128 : (h + 1) * 128] = factor(li, line(col[h], s, 32))
        li = jnp.take_along_axis(line(of_third, s, 8), spread, axis=1)
        for e in range(2):
            ang_pair[s, e] = factor(li, line(col[2 + e], s, 8))


def gather_kernel(wave_in, labels_in, rows_in, cols_in, owners_in, kt_in, w_all, roles, ang, ang_pair, kt,
                  b0, b1, b2, meta, table, via_x, via_y, wave, labels, rows, cols, owners, in_sem,
                  z_send, z_recv, c_send, c_recv, m_send, m_recv):
    loads = [
        pltpu.make_async_copy(src, dst, in_sem.at[k])
        for k, (src, dst) in enumerate(
            ((wave_in, wave), (labels_in, labels), (rows_in, rows), (cols_in, cols), (owners_in, owners), (kt_in, kt))
        )
    ]
    for load in loads:
        load.start()
    own, own_d = lax.axis_index("bin"), lax.axis_index("dist")
    x, yh, core = own // 4, (own // 2) % 2, own % 2
    z, yl = own_d // 2, own_d % 2
    y = yh * 2 + yl
    other = 1 - core

    def chip(px, py, pz, pc):
        return (px * 4 + (py // 2) * 2 + pc, pz * 2 + py % 2)

    def up(v, o):
        return (v + o) % 4

    def peer(axis, o):
        return chip(
            up(x, o) if axis == "x" else x, up(y, o) if axis == "y" else y, up(z, o) if axis == "z" else z, core
        )

    barrier = pltpu.get_barrier_semaphore()
    peers = [peer(axis, o) for o in (2, 1, 3) for axis in "xyz"] + [chip(x, y, z, other)]
    for at in peers:
        pl.semaphore_signal(barrier, inc=1, device_id=at, device_id_type=MESH)

    loads[0].wait()
    shard = wave[...].astype(F32).T
    for rt, b in enumerate((b0, b1, b2)):
        part = jnp.concatenate(
            [shard[rt * 32 : rt * 32 + 16, :], shard[rt * 32 + 16 : rt * 32 + 32, :]], axis=1
        ).astype(BF)
        if rt == 0:
            b[core, x, y, z] = part
        elif rt == 1:
            b[core, z, x, y] = part
        else:
            b[core, y, z, x] = part

    pl.semaphore_wait(barrier, len(peers))

    def copy(src, dst, send, recv, device):
        return pltpu.make_async_remote_copy(
            src_ref=src, dst_ref=dst, send_sem=send, recv_sem=recv, device_id=device, device_id_type=MESH
        )

    def taken(ref, send):
        copy(ref, ref, send, send, peers[0]).wait_send()

    def arrived(ref, recv):
        copy(ref, ref, recv, recv, peers[0]).wait_recv()

    def block(rt, stage, v, c):
        if rt == 0:
            return (b0.at[c, x, y, v], b0.at[c, x, v], b0.at[c, v])[stage]
        if rt == 1:
            return (b1.at[c, z, x, v], b1.at[c, z, v], b1.at[c, v])[stage]
        return (b2.at[c, y, z, v], b2.at[c, y, v], b2.at[c, v])[stage]

    def place(rt, stage):
        axis = ("zyx", "yxz", "xzy")[rt][stage]
        return {"x": x, "y": y, "z": z}[axis], axis

    def push(rt, stage):
        at, axis = place(rt, stage)
        mine = block(rt, stage, at, core)
        for o in (2, 1, 3):
            recv = z_recv.at[rt, stage + (stage == 2 and o == 2)]
            copy(mine, mine, z_send.at[rt, stage], recv, peer(axis, o)).start()

    def some(rt, stage, n):
        b = (b0, b1, b2)[rt]
        return (b.at[0, 0, 0, pl.ds(0, n)], b.at[0, 0, pl.ds(0, n)], b.at[0, pl.ds(0, n)])[stage]

    def across(rt, o, k):
        v = up(place(rt, 2)[0], (4 - o) % 4)
        copy(block(rt, 2, v, core), block(rt, 2, v, core), c_send.at[rt], c_recv.at[rt, k], chip(x, y, z, other)).start()

    def lay_stage(rt, c, o):
        if rt < 2:
            lay_plane(rt, up(place(rt, 2)[0], (4 - o) % 4), c)

    def lay(rt, c, px, h, pz, even, odd):
        tile = rt * 16 + c * 8 + h * 4 + px
        lanes = pl.ds(pl.multiple_of(pz * 128, 128), 128)
        w_all[tile, 0:16, lanes] = jnp.concatenate([even[:, :64], odd[:, :64]], axis=1)
        w_all[tile, 16:32, lanes] = jnp.concatenate([even[:, 64:], odd[:, 64:]], axis=1)

    def lay_plane(rt, v, c):
        if rt == 0:
            for h in range(2):
                for pz in range(4):
                    lay(0, c, v, h, pz, b0[c, v, 2 * h, pz], b0[c, v, 2 * h + 1, pz])
        elif rt == 1:
            for px in range(4):
                for h in range(2):
                    lay(1, c, px, h, v, b1[c, v, px, 2 * h], b1[c, v, px, 2 * h + 1])
        else:
            for pz in range(4):
                for px in range(4):
                    lay(2, c, px, v, pz, b2[c, 2 * v, pz, px], b2[c, 2 * v + 1, pz, px])

    for rt in range(RPT):
        push(rt, 0)

    for load in loads[1:]:
        load.wait()
    sub64 = lax.broadcasted_iota(jnp.int32, (64, 64), 0)
    lan64 = lax.broadcasted_iota(jnp.int32, (64, 64), 1)

    def column(row):
        return jnp.sum(jnp.where(sub64 == lan64, jnp.broadcast_to(row, (64, 64)), 0), axis=1, keepdims=True)

    own_r, col_r = owners[...], cols[...]
    own_c = column(own_r)
    same = (jnp.broadcast_to(own_c, (64, 64)) == own_r) & (lan64 < sub64)
    slot_c = jnp.sum(jnp.where(same, 1, 0), axis=1, keepdims=True)
    third = lax.shift_right_logical(col_r * 171, 9)
    number = (third & 1) * 8 + (third & 2) * 2 + lax.shift_right_logical(third, 2)
    code_c = column(1 + rows[...] * 64 + (col_r - 3 * third) * 16 + number)
    lane64 = lax.broadcasted_iota(jnp.int32, (64, 128), 1)
    lane1 = lax.broadcasted_iota(jnp.int32, (1, 128), 1)
    spread = jnp.where(lane64 == slot_c, jnp.broadcast_to(code_c, (64, 128)), 0)
    label_row = jnp.concatenate([jnp.zeros((1, 32), jnp.int32), labels[...]], axis=1)
    for o in range(NS):
        mine = jnp.where(own_c == o, spread, 0)
        table[o // 4, o % 4] = jnp.where(lane1 < 32, jnp.sum(mine, axis=0, keepdims=True), label_row)

    for o in (2, 1, 3):
        copy(table.at[up(x, o)], via_x.at[x], m_send.at[0], m_recv.at[0], peer("x", o)).start()
    via_x[x] = table[x]

    for rt in range(RPT):
        arrived(some(rt, 0, 3), z_recv.at[rt, 0])
        push(rt, 1)
    for rt in range(RPT):
        taken(some(rt, 0, 3), z_send.at[rt, 0])

    arrived(via_x.at[pl.ds(0, 3)], m_recv.at[0])
    taken(table.at[pl.ds(0, 3)], m_send.at[0])
    far = 1 - yh
    meta_y = copy(via_x.at[:, pl.ds(far * 2, 2)], via_y.at[yh], m_send.at[1], m_recv.at[1], peer("y", 2))
    meta_y.start()
    via_y[yh] = via_x[:, pl.ds(yh * 2, 2)]

    for rt in range(RPT):
        arrived(some(rt, 1, 3), z_recv.at[rt, 1])
        push(rt, 2)
        across(rt, 0, 0)
    for rt in range(RPT):
        taken(some(rt, 1, 3), z_send.at[rt, 1])

    arrived(via_y.at[far], m_recv.at[1])
    meta_c = copy(via_y.at[:, :, other], meta.at[core], m_send.at[2], m_recv.at[2], chip(x, y, z, other))
    meta_c.start()
    meta_y.wait_send()
    meta[core] = via_y[:, :, core]
    w_all[48] = jnp.zeros((32, 512), BF)
    lay_plane(0, x, core)
    lay_plane(1, z, core)

    arrived(meta.at[other], m_recv.at[2])
    meta_c.wait_send()
    tables(meta, roles, ang, ang_pair)
    for rt in range(RPT):
        arrived(some(rt, 2, 2), z_recv.at[rt, 2])
        across(rt, 1, 1)
        across(rt, 3, 1)
    for rt in range(RPT):
        arrived(some(rt, 2, 1), c_recv.at[rt, 0])
        lay_stage(rt, other, 0)
        lay_stage(rt, core, 1)
        lay_stage(rt, core, 3)
    lay_plane(2, yh, core)
    for rt in range(RPT):
        arrived(some(rt, 2, 1), z_recv.at[rt, 3])
        across(rt, 2, 2)
    for rt in range(RPT):
        arrived(some(rt, 2, 2), c_recv.at[rt, 1])
        lay_stage(rt, other, 1)
        lay_stage(rt, other, 3)
        lay_stage(rt, core, 2)
    lay_plane(2, yh, other)
    lay_plane(2, far, core)
    for rt in range(RPT):
        taken(some(rt, 2, 3), z_send.at[rt, 2])
    for rt in range(RPT):
        arrived(some(rt, 2, 1), c_recv.at[rt, 2])
        lay_stage(rt, other, 2)
    lay_plane(2, far, other)
    for rt in range(RPT):
        taken(some(rt, 2, 4), c_send.at[rt])


def swap_blocks(lane, x):
    half, even = lane

    def mixed(a, b, c, d):
        ab, cd = jnp.where(even, a, b), jnp.where(even, c, d)
        return jnp.where(half, ab, cd), jnp.where(half, cd, ab)

    z0, z2 = mixed(x[0], x[1], x[2], x[3])
    z1, z3 = mixed(x[3], x[0], x[1], x[2])
    u = z0, pltpu.roll(z1, 96, 1), pltpu.roll(z2, 64, 1), pltpu.roll(z3, 32, 1)
    y0, y2 = mixed(u[0], u[3], u[2], u[1])
    y1, y3 = mixed(u[1], u[0], u[3], u[2])
    return y0, y1, y2, y3


CHUNKS = ((0, 6), (6, 12), (12, 17), (17, 22), (22, 27), (27, 32))
STEPS = ((0, 0), 0, (0, 1), (1, 1), 1, (1, 0), 2, (2, 0), 3, (2, 1), (3, 1), 4, (3, 0), 5, (4, 0), 6, (4, 1), (5, 1), 7, (5, 0))


def loads_weights(k):
    return isinstance(STEPS[k], int) or isinstance(STEPS[k - 1], int) or k == 0 or STEPS[k][1] != STEPS[k - 1][1]


WIDE = [k for k, step in enumerate(STEPS) if not isinstance(step, int) and loads_weights(k)]


def forms_kernel(roles, W, ANG, ANGP, kt_ref, out, OUT, cols_first, cols_second, sem):
    place = lax.broadcasted_iota(jnp.int32, (16, 128), 1) // 32
    lane_f = (place // 2).astype(F32).astype(BF), (place % 2).astype(F32).astype(BF)
    def halves(m):
        return slice(m * 256, (m + 1) * 256)

    def turn(s, which):
        cols = jnp.concatenate([W[roles[s, 0, TILES + 8 * which + n]] for n in range(CAP)], axis=0)
        (cols_first, cols_second)[which][...] = cols.T

    def push_wide(which):
        cols = (cols_first, cols_second)[which]
        for m in range(2):
            pltpu.matmul_push_rhs(cols[halves(m), :], 0, m)

    def push_pair(s, j):
        e, u, kh = j // 4, (j // 2) % 2, j % 2
        rows = W.at[roles[s, 0, ROW + 2]]
        cols = W[roles[s, 0, PAIR_TILE + e], :, halves(kh)]
        for m in range(2):
            at = (u * 2 + m) * 8
            pair = jnp.concatenate([rows[i : i + 1, halves(kh)] * cols for i in range(at, at + 8)], axis=0)
            pltpu.matmul_push_rhs(pair, 1, m, transpose=True)

    def whole(*flat):
        wide = [[flat[m * 16 + b * 6 : m * 16 + b * 6 + 6] for b in range(2)] for m in range(2)]
        narrow = [flat[m * 16 + 12 : m * 16 + 16] for m in range(2)]

        def step(s, k, nxt):
            what = STEPS[k]
            if isinstance(what, int):
                kh = what % 2
                for m in range(2):
                    pltpu.matmul_acc_lhs(narrow[m][what // 2], kt_ref[:, halves(kh)], load_staged_rhs=1)
                push_pair(s if what < 7 else nxt, (what + 1) % 8)
                return
            c, which = what
            row = roles[s, 0, ROW + which]
            lo, hi = CHUNKS[c]
            for u in range(lo, hi):
                g, db = u // 4, u % 4
                kt = kt_ref[db * 16 : (db + 1) * 16, :]
                if u == lo or db == 0:
                    wide_rows = [jnp.broadcast_to(W[row, i : i + 1, :], (16, 512)) for i in range(g * 4, g * 4 + 4)]
                lhs = jnp.concatenate([r * kt for r in wide_rows], axis=0)
                load = u == lo and loads_weights(k)
                for m in range(2):
                    pltpu.matmul_acc_lhs(wide[m][c % 2][u - lo], lhs[:, halves(m)], load_staged_rhs=0 if load else None)
                if load:
                    at = WIDE.index(k) + 1
                    if at == len(WIDE):
                        turn(nxt, 0)
                    push_wide(STEPS[WIDE[at % len(WIDE)]][1])
                    if at == len(WIDE) - 1:
                        turn(nxt, 1)

        def post_wide(s, c, part, dest):
            buf = s % 2
            lo, hi = CHUNKS[c]
            mid = lo + (hi - lo + 1) // 2
            for u in range(lo, mid) if part == 0 else range(mid, hi):
                g, db = u // 4, u % 4
                f = pltpu.matmul_pop(wide[0][c % 2][u - lo]) + pltpu.matmul_pop(wide[1][c % 2][u - lo])
                low, high = [], []
                for i4 in range(4):
                    i = g * 4 + i4
                    v = (f[i4 * 16 : (i4 + 1) * 16, :] * ANG[s, i : i + 1, :]).astype(BF)
                    low.append(v[:, :128])
                    high.append(v[:, 128:])
                for base, xs in ((0, low), (4, high)):
                    for n, v in enumerate(swap_blocks((lane_f[0] < 0.5, lane_f[1] < 0.5), xs)):
                        OUT[buf, dest[base + n], db * 16 : (db + 1) * 16, g * 128 : (g + 1) * 128] = v

        def post_pair(s, j):
            buf = s % 2
            e, u = j // 4, (j // 2) % 2
            for m in range(2):
                nt = u * 2 + m
                f = pltpu.matmul_pop(narrow[m][j // 2])
                for h in range(2):
                    g = nt * 2 + h
                    v = f[:, h * 128 : (h + 1) * 128] * ANGP[s, e, g : g + 1, :]
                    OUT[buf, roles[s, 0, PAIR + e], :, g * 128 : (g + 1) * 128] = v.astype(BF)

        def copy(s):
            place = (s % 4) * 4 + ((s // 4) % 2) * 2 + s // 8
            return pltpu.make_async_copy(OUT.at[s % 2, pl.ds(0, CAP)], out.at[pl.ds(place * CAP, CAP)], sem.at[s % 2])

        turn(0, 0)
        turn(0, 1)
        push_wide(0)
        push_pair(0, 0)
        step(0, 0, 0)

        def sender(s, _):
            nxt = jnp.minimum(s + 1, NS - 1)
            dest = [roles[s, 0, DEST + n] for n in range(CAP)]

            @pl.when(s >= 2)
            def _():
                copy(s - 2).wait()

            for k in range(1, len(STEPS) + 1):
                if k < len(STEPS):
                    step(s, k, nxt)
                    what = STEPS[k]
                else:
                    step(nxt, 0, nxt)
                    what = (6, 0)
                if isinstance(what, int):
                    continue
                done = STEPS[k - 1]
                if isinstance(done, int) and done % 2 == 1 and k < len(STEPS):
                    post_pair(s, done)
                c = what[0]
                if c > 0:
                    first = not any(not isinstance(w, int) and w[0] == c for w in STEPS[:k])
                    post_wide(s, c - 1, 0 if first else 1, dest)
            post_wide(s, 5, 1, dest)
            copy(s).start()
            return 0

        lax.fori_loop(0, NS, sender, 0)
        left = jnp.zeros((64, 256), F32)
        for m in range(2):
            pltpu.matmul_acc_lhs(wide[m][0][0], kt_ref[:, halves(m)], load_staged_rhs=0)
            pltpu.matmul_acc_lhs(narrow[m][0], kt_ref[:, halves(m)], load_staged_rhs=1)
            for acc in (*wide[m][0], narrow[m][0]):
                left = left + pltpu.matmul_pop(acc)
        OUT[0, CAP, :, 0:256] = left.astype(BF)
        copy(NS - 2).wait()
        copy(NS - 1).wait()

    pl.run_scoped(whole, *[pltpu.ACC(m)((64, 256), F32) for m in range(2) for _ in range(16)])


def gather(wave, labels, rows, cols, owners, kt):
    vm = pl.BlockSpec(memory_space=pltpu.VMEM)
    blocks = pltpu.VMEM((2, 4, 4, 4, 16, 128), BF)
    i32 = jnp.int32
    dma = pltpu.SemaphoreType.DMA
    return pl.pallas_call(
        gather_kernel,
        in_specs=[pl.BlockSpec(memory_space=pltpu.HBM)] * 6,
        out_specs=[vm] * 5,
        out_shape=[
            jax.ShapeDtypeStruct((49, 32, 512), BF),
            jax.ShapeDtypeStruct((NS, 1, 128), i32),
            jax.ShapeDtypeStruct((NS, 32, 256), F32),
            jax.ShapeDtypeStruct((NS, 2, 8, 128), F32),
            jax.ShapeDtypeStruct((D, 512), BF),
        ],
        scratch_shapes=[
            blocks, blocks, blocks,
            pltpu.VMEM((2, 2, 4, 1, 128), i32),
            pltpu.VMEM((4, 4, 1, 128), i32),
            pltpu.VMEM((4, 4, 1, 128), i32),
            pltpu.VMEM((2, 4, 2, 1, 128), i32),
            pltpu.VMEM((64, 96), BF),
            pltpu.VMEM((1, 96), i32),
            pltpu.VMEM((1, 64), i32),
            pltpu.VMEM((1, 64), i32),
            pltpu.VMEM((1, 64), i32),
            dma((6,)),
            dma((3, 3)), dma((3, 4)), dma((3,)), dma((3, 3)), dma((3,)), dma((3,)),
        ],
        compiler_params=pltpu.CompilerParams(
            collective_id=0, has_side_effects=True, vmem_limit_bytes=24 * 2**20
        ),
    )(wave, labels, rows, cols, owners, kt)


def forms(roles, w_all, ang, ang_pair, kt):
    vm = pl.BlockSpec(memory_space=pltpu.VMEM)
    return pl.pallas_call(
        forms_kernel,
        in_specs=[pl.BlockSpec(memory_space=pltpu.SMEM), vm, vm, vm, vm],
        out_specs=pl.BlockSpec(memory_space=pltpu.HBM),
        out_shape=jax.ShapeDtypeStruct((NS * CAP, D, 1024), BF),
        scratch_shapes=[
            pltpu.VMEM((2, CAP + 1, D, 1024), BF),
            pltpu.VMEM((512, 256), BF),
            pltpu.VMEM((512, 256), BF),
            pltpu.SemaphoreType.DMA((2,)),
        ],
        compiler_params=pltpu.CompilerParams(vmem_limit_bytes=40 * 2**20),
    )(roles, w_all, ang, ang_pair, kt)


def per_device(wavefuncs, kernel, labels, row_tiles, col_tiles, owners):
    def in_hbm(v):
        return pltpu.with_memory_space_constraint(v, pltpu.HBM)

    w_all, roles, ang, ang_pair, kt = gather(
        in_hbm(wavefuncs.T),
        in_hbm(labels.reshape(1, 96)),
        in_hbm(row_tiles.reshape(1, 64)),
        in_hbm(col_tiles.reshape(1, 64)),
        in_hbm(owners.T),
        in_hbm(kernel.T),
    )
    return forms(roles, w_all, ang, ang_pair, kt)


def solution(mesh):
    return jax.shard_map(
        per_device,
        mesh=mesh,
        in_specs=(P("bin", "dist"), P(None, "dist"), P("bin"), P("bin"), P("bin"), P("bin", None)),
        out_specs=P("bin", "dist", None),
        check_vma=False,
    )
```

```python
import functools
import jax
import jax.numpy as jnp
from jax import lax
from jax.experimental import pallas as pl
from jax.experimental.pallas import tpu as pltpu
from jax.sharding import PartitionSpec as P

D = 64
RPT = 3
CAP = 8
NS = 16
BF = jnp.bfloat16
F32 = jnp.float32
MESH = pl.DeviceIdType.MESH


TILES, DEST, ROW, PAIR, PAIR_TILE = 0, 16, 24, 27, 29


def factor(li, lj):
    return jnp.sqrt((2.0 * li + 1.0) * (2.0 * lj + 1.0)) / (8.0 * (1.0 + jnp.abs(li - lj)))


def tables(meta, roles, ang, ang_pair):
    lane = lax.broadcasted_iota(jnp.int32, (NS, 128), 1)
    sender = lax.broadcasted_iota(jnp.int32, (NS, 128), 0)
    found = jnp.concatenate([meta[c, h, p] for c in range(2) for h in range(2) for p in range(4)], axis=0)
    ok = (found > 0) & (lane < CAP)
    at = jnp.maximum(found - 1, 0)
    row, tile = at >> 6, at & 63

    def total(mask, value):
        return jnp.sum(jnp.where(mask, value, 0), axis=1, keepdims=True)

    n = [total(ok & (row == r), 1) for r in range(RPT)]
    third = jnp.where((n[0] <= n[1]) & (n[0] <= n[2]), 0, jnp.where(n[1] <= n[2], 1, 2))
    first = jnp.where(third == 0, 1, 0)
    second = jnp.where(third == 2, 1, 2)
    single = ok & (row == third)
    p0 = jnp.min(jnp.where(single, lane, CAP), axis=1, keepdims=True)
    p1 = jnp.max(jnp.where(single, lane, -1), axis=1, keepdims=True)
    p1 = jnp.where((p1 == p0) | (p1 < 0), CAP, p1)
    t0 = jnp.where(p0 < CAP, total(single & (lane == p0), tile), 48)
    t1 = jnp.where(p1 < CAP, total(single & (lane == p1), tile), 48)
    role = jnp.where(ok & (row == first), tile, 48)
    role = jnp.where(lane < 8, role, pltpu.roll(jnp.where(ok & (row == second), tile, 48), 8, 1))
    role = jnp.where(lane < 16, role, pltpu.roll(jnp.where(single, CAP, lane), 16, 1))
    for k, v in enumerate((first * 16 + sender, second * 16 + sender, third * 16 + sender, p0, p1, t0, t1)):
        role = jnp.where(lane == ROW + k, v, role)
    for s in range(NS):
        roles[s] = role[s : s + 1, :]

    real = found.astype(F32)
    rolled = [real] + [pltpu.roll(real, 32 * k, 1) for k in (1, 2, 3)]
    labels = []
    for rt in range(RPT):
        v = rolled[(0 - rt - 1) % 4]
        for g in (1, 2, 3):
            v = jnp.where(lane // 32 == g, rolled[(g - rt - 1) % 4], v)
        labels.append(v)
    row_of = [jnp.take_along_axis(row, lane // 32 + 4 * h, axis=1) for h in range(2)]
    tile_of = [jnp.take_along_axis(tile, lane // 32 + 4 * h, axis=1) for h in range(2)]
    tile_of += [jnp.broadcast_to(t, (NS, 128)) for t in (t0, t1)]
    col = [jnp.zeros((NS, 128), F32) for _ in tile_of]
    for t in range(48):
        of = jnp.broadcast_to(labels[t // 16][t % 16 : t % 16 + 1, :], (NS, 128))
        col = [jnp.where(which == t, of, v) for which, v in zip(tile_of, col)]
    of_third = jnp.where(third == 0, labels[0], jnp.where(third == 1, labels[1], labels[2]))
    lane32 = lax.broadcasted_iota(jnp.int32, (32, 128), 1)
    eye = lane32 == lax.broadcasted_iota(jnp.int32, (32, 128), 0)
    spread = lax.broadcasted_iota(jnp.int32, (8, 128), 0) * 4 + lax.broadcasted_iota(jnp.int32, (8, 128), 1) // 32

    def line(v, s, rows):
        return jnp.broadcast_to(v[s : s + 1, :], (rows, 128))

    for s in range(NS):
        down = [jnp.sum(jnp.where(eye, line(labels[rt], s, 32), 0.0), axis=1, keepdims=True) for rt in range(RPT)]
        for h in range(2):
            r = line(row_of[h], s, 32)
            li = jnp.where(r == 0, down[0], jnp.where(r == 1, down[1], down[2]))
            ang[s, :, h * 128 : (h + 1) * 128] = factor(li, line(col[h], s, 32))
        li = jnp.take_along_axis(line(of_third, s, 8), spread, axis=1)
        for e in range(2):
            ang_pair[s, e] = factor(li, line(col[2 + e], s, 8))


def gather_kernel(wave_in, labels_in, rows_in, cols_in, owners_in, kt_in, w_all, roles, ang, ang_pair, kt,
                  b0, b1, b2, meta, table, via_x, via_y, wave, labels, rows, cols, owners, in_sem,
                  z_send, z_recv, c_send, c_recv, m_send, m_recv):
    loads = [
        pltpu.make_async_copy(src, dst, in_sem.at[k])
        for k, (src, dst) in enumerate(
            ((wave_in, wave), (labels_in, labels), (rows_in, rows), (cols_in, cols), (owners_in, owners), (kt_in, kt))
        )
    ]
    for load in loads:
        load.start()
    own, own_d = lax.axis_index("bin"), lax.axis_index("dist")
    x, yh, core = own // 4, (own // 2) % 2, own % 2
    z, yl = own_d // 2, own_d % 2
    y = yh * 2 + yl
    other = 1 - core

    def chip(px, py, pz, pc):
        return (px * 4 + (py // 2) * 2 + pc, pz * 2 + py % 2)

    def up(v, o):
        return (v + o) % 4

    def peer(axis, o):
        return chip(
            up(x, o) if axis == "x" else x, up(y, o) if axis == "y" else y, up(z, o) if axis == "z" else z, core
        )

    def diagonal(axis, o, axis2, o2):
        by = {axis: o, axis2: o2}
        return chip(up(x, by.get("x", 0)), up(y, by.get("y", 0)), up(z, by.get("z", 0)), core)

    barrier = pltpu.get_barrier_semaphore()
    peers = [peer(axis, o) for o in (2, 1, 3) for axis in "xyz"] + [chip(x, y, z, other)]
    peers += [diagonal(p, o, q, o2) for p, q in ("zy", "yx", "xz") for o in (2, 1, 3) for o2 in (2, 1, 3)]
    for at in peers:
        pl.semaphore_signal(barrier, inc=1, device_id=at, device_id_type=MESH)

    loads[0].wait()
    shard = wave[...].astype(F32).T
    for rt, b in enumerate((b0, b1, b2)):
        part = jnp.concatenate(
            [shard[rt * 32 : rt * 32 + 16, :], shard[rt * 32 + 16 : rt * 32 + 32, :]], axis=1
        ).astype(BF)
        if rt == 0:
            b[core, x, y, z] = part
        elif rt == 1:
            b[core, z, x, y] = part
        else:
            b[core, y, z, x] = part

    pl.semaphore_wait(barrier, len(peers))

    def copy(src, dst, send, recv, device):
        return pltpu.make_async_remote_copy(
            src_ref=src, dst_ref=dst, send_sem=send, recv_sem=recv, device_id=device, device_id_type=MESH
        )

    def taken(ref, send):
        copy(ref, ref, send, send, peers[0]).wait_send()

    def arrived(ref, recv):
        copy(ref, ref, recv, recv, peers[0]).wait_recv()

    def block(rt, stage, v, c):
        if rt == 0:
            return (b0.at[c, x, y, v], b0.at[c, x, v], b0.at[c, v])[stage]
        if rt == 1:
            return (b1.at[c, z, x, v], b1.at[c, z, v], b1.at[c, v])[stage]
        return (b2.at[c, y, z, v], b2.at[c, y, v], b2.at[c, v])[stage]

    def place(rt, stage):
        axis = ("zyx", "yxz", "xzy")[rt][stage]
        return {"x": x, "y": y, "z": z}[axis], axis

    def push(rt, stage):
        at, axis = place(rt, stage)
        mine = block(rt, stage, at, core)
        for o in (2, 1, 3):
            recv = z_recv.at[rt, stage + (stage == 2 and o == 2)]
            copy(mine, mine, z_send.at[rt, stage], recv, peer(axis, o)).start()

    def some(rt, stage, n):
        b = (b0, b1, b2)[rt]
        return (b.at[0, 0, 0, pl.ds(0, n)], b.at[0, 0, pl.ds(0, n)], b.at[0, pl.ds(0, n)])[stage]

    def across(rt, o, k):
        v = up(place(rt, 2)[0], (4 - o) % 4)
        copy(block(rt, 2, v, core), block(rt, 2, v, core), c_send.at[rt], c_recv.at[rt, k], chip(x, y, z, other)).start()

    def lay_stage(rt, c, o):
        if rt < 2:
            lay_plane(rt, up(place(rt, 2)[0], (4 - o) % 4), c)

    def lay(rt, c, px, h, pz, even, odd):
        tile = rt * 16 + c * 8 + h * 4 + px
        lanes = pl.ds(pl.multiple_of(pz * 128, 128), 128)
        w_all[tile, 0:16, lanes] = jnp.concatenate([even[:, :64], odd[:, :64]], axis=1)
        w_all[tile, 16:32, lanes] = jnp.concatenate([even[:, 64:], odd[:, 64:]], axis=1)

    def lay_plane(rt, v, c):
        if rt == 0:
            for h in range(2):
                for pz in range(4):
                    lay(0, c, v, h, pz, b0[c, v, 2 * h, pz], b0[c, v, 2 * h + 1, pz])
        elif rt == 1:
            for px in range(4):
                for h in range(2):
                    lay(1, c, px, h, v, b1[c, v, px, 2 * h], b1[c, v, px, 2 * h + 1])
        else:
            for pz in range(4):
                for px in range(4):
                    lay(2, c, px, v, pz, b2[c, 2 * v, pz, px], b2[c, 2 * v + 1, pz, px])

    for o, o2 in [(a, b) for a in (2, 1, 3, 0) for b in (2, 1, 3, 0) if a or b]:
        for rt, (p, q) in enumerate(("zy", "yx", "xz")):
            mine = block(rt, 0, place(rt, 0)[0], core)
            copy(mine, mine, z_send.at[rt, 0], z_recv.at[rt, 1 if o2 else 0], diagonal(p, o, q, o2)).start()

    for load in loads[1:]:
        load.wait()
    sub64 = lax.broadcasted_iota(jnp.int32, (64, 64), 0)
    lan64 = lax.broadcasted_iota(jnp.int32, (64, 64), 1)

    def column(row):
        return jnp.sum(jnp.where(sub64 == lan64, jnp.broadcast_to(row, (64, 64)), 0), axis=1, keepdims=True)

    own_r, col_r = owners[...], cols[...]
    own_c = column(own_r)
    same = (jnp.broadcast_to(own_c, (64, 64)) == own_r) & (lan64 < sub64)
    slot_c = jnp.sum(jnp.where(same, 1, 0), axis=1, keepdims=True)
    third = lax.shift_right_logical(col_r * 171, 9)
    number = (third & 1) * 8 + (third & 2) * 2 + lax.shift_right_logical(third, 2)
    code_c = column(1 + rows[...] * 64 + (col_r - 3 * third) * 16 + number)
    lane64 = lax.broadcasted_iota(jnp.int32, (64, 128), 1)
    lane1 = lax.broadcasted_iota(jnp.int32, (1, 128), 1)
    spread = jnp.where(lane64 == slot_c, jnp.broadcast_to(code_c, (64, 128)), 0)
    label_row = jnp.concatenate([jnp.zeros((1, 32), jnp.int32), labels[...]], axis=1)
    for o in range(NS):
        mine = jnp.where(own_c == o, spread, 0)
        table[o // 4, o % 4] = jnp.where(lane1 < 32, jnp.sum(mine, axis=0, keepdims=True), label_row)

    for o in (2, 1, 3):
        copy(table.at[up(x, o)], via_x.at[x], m_send.at[0], m_recv.at[0], peer("x", o)).start()
    via_x[x] = table[x]


    arrived(via_x.at[pl.ds(0, 3)], m_recv.at[0])
    taken(table.at[pl.ds(0, 3)], m_send.at[0])
    far = 1 - yh
    meta_y = copy(via_x.at[:, pl.ds(far * 2, 2)], via_y.at[yh], m_send.at[1], m_recv.at[1], peer("y", 2))
    meta_y.start()
    via_y[yh] = via_x[:, pl.ds(yh * 2, 2)]

    for rt in range(RPT):
        arrived(some(rt, 0, 3), z_recv.at[rt, 0])
        arrived(some(rt, 1, 3), z_recv.at[rt, 1])
        push(rt, 2)
        across(rt, 0, 0)
    for rt in range(RPT):
        taken(some(rt, 0, 3), z_send.at[rt, 0])
        taken(some(rt, 1, 3), z_send.at[rt, 0])

    arrived(via_y.at[far], m_recv.at[1])
    meta_c = copy(via_y.at[:, :, other], meta.at[core], m_send.at[2], m_recv.at[2], chip(x, y, z, other))
    meta_c.start()
    meta_y.wait_send()
    meta[core] = via_y[:, :, core]
    w_all[48] = jnp.zeros((32, 512), BF)
    lay_plane(0, x, core)
    lay_plane(1, z, core)

    arrived(meta.at[other], m_recv.at[2])
    meta_c.wait_send()
    tables(meta, roles, ang, ang_pair)
    for rt in range(RPT):
        arrived(some(rt, 2, 2), z_recv.at[rt, 2])
        across(rt, 1, 1)
        across(rt, 3, 1)
    for rt in range(RPT):
        arrived(some(rt, 2, 1), c_recv.at[rt, 0])
        lay_stage(rt, other, 0)
        lay_stage(rt, core, 1)
        lay_stage(rt, core, 3)
    lay_plane(2, yh, core)
    for rt in range(RPT):
        arrived(some(rt, 2, 1), z_recv.at[rt, 3])
        across(rt, 2, 2)
    for rt in range(RPT):
        arrived(some(rt, 2, 2), c_recv.at[rt, 1])
        lay_stage(rt, other, 1)
        lay_stage(rt, other, 3)
        lay_stage(rt, core, 2)
    lay_plane(2, yh, other)
    lay_plane(2, far, core)
    for rt in range(RPT):
        taken(some(rt, 2, 3), z_send.at[rt, 2])
    for rt in range(RPT):
        arrived(some(rt, 2, 1), c_recv.at[rt, 2])
        lay_stage(rt, other, 2)
    lay_plane(2, far, other)
    for rt in range(RPT):
        taken(some(rt, 2, 4), c_send.at[rt])


def swap_blocks(lane, x):
    half, even = lane

    def mixed(a, b, c, d):
        ab, cd = jnp.where(even, a, b), jnp.where(even, c, d)
        return jnp.where(half, ab, cd), jnp.where(half, cd, ab)

    z0, z2 = mixed(x[0], x[1], x[2], x[3])
    z1, z3 = mixed(x[3], x[0], x[1], x[2])
    u = z0, pltpu.roll(z1, 96, 1), pltpu.roll(z2, 64, 1), pltpu.roll(z3, 32, 1)
    y0, y2 = mixed(u[0], u[3], u[2], u[1])
    y1, y3 = mixed(u[1], u[0], u[3], u[2])
    return y0, y1, y2, y3


CHUNKS = ((0, 6), (6, 12), (12, 17), (17, 22), (22, 27), (27, 32))
STEPS = ((0, 0), 0, (0, 1), (1, 1), 1, (1, 0), 2, (2, 0), 3, (2, 1), (3, 1), 4, (3, 0), 5, (4, 0), 6, (4, 1), (5, 1), 7, (5, 0))


def loads_weights(k):
    return isinstance(STEPS[k], int) or isinstance(STEPS[k - 1], int) or k == 0 or STEPS[k][1] != STEPS[k - 1][1]


WIDE = [k for k, step in enumerate(STEPS) if not isinstance(step, int) and loads_weights(k)]


def forms_kernel(roles, W, ANG, ANGP, kt_ref, out, OUT, cols_first, cols_second, sem):
    place = lax.broadcasted_iota(jnp.int32, (16, 128), 1) // 32
    lane_f = (place // 2).astype(F32).astype(BF), (place % 2).astype(F32).astype(BF)
    def halves(m):
        return slice(m * 256, (m + 1) * 256)

    def turn(s, which):
        cols = jnp.concatenate([W[roles[s, 0, TILES + 8 * which + n]] for n in range(CAP)], axis=0)
        (cols_first, cols_second)[which][...] = cols.T

    def push_wide(which):
        cols = (cols_first, cols_second)[which]
        for m in range(2):
            pltpu.matmul_push_rhs(cols[halves(m), :], 0, m)

    def push_pair(s, j):
        e, u, kh = j // 4, (j // 2) % 2, j % 2
        rows = W.at[roles[s, 0, ROW + 2]]
        cols = W[roles[s, 0, PAIR_TILE + e], :, halves(kh)]
        for m in range(2):
            at = (u * 2 + m) * 8
            pair = jnp.concatenate([rows[i : i + 1, halves(kh)] * cols for i in range(at, at + 8)], axis=0)
            pltpu.matmul_push_rhs(pair, 1, m, transpose=True)

    def whole(*flat):
        wide = [[flat[m * 16 + b * 6 : m * 16 + b * 6 + 6] for b in range(2)] for m in range(2)]
        narrow = [flat[m * 16 + 12 : m * 16 + 16] for m in range(2)]

        def step(s, k, nxt):
            what = STEPS[k]
            if isinstance(what, int):
                kh = what % 2
                for m in range(2):
                    pltpu.matmul_acc_lhs(narrow[m][what // 2], kt_ref[:, halves(kh)], load_staged_rhs=1)
                push_pair(s if what < 7 else nxt, (what + 1) % 8)
                return
            c, which = what
            row = roles[s, 0, ROW + which]
            lo, hi = CHUNKS[c]
            for u in range(lo, hi):
                g, db = u // 4, u % 4
                kt = kt_ref[db * 16 : (db + 1) * 16, :]
                if u == lo or db == 0:
                    wide_rows = [jnp.broadcast_to(W[row, i : i + 1, :], (16, 512)) for i in range(g * 4, g * 4 + 4)]
                lhs = jnp.concatenate([r * kt for r in wide_rows], axis=0)
                load = u == lo and loads_weights(k)
                for m in range(2):
                    pltpu.matmul_acc_lhs(wide[m][c % 2][u - lo], lhs[:, halves(m)], load_staged_rhs=0 if load else None)
                if load:
                    at = WIDE.index(k) + 1
                    if at == len(WIDE):
                        turn(nxt, 0)
                    push_wide(STEPS[WIDE[at % len(WIDE)]][1])
                    if at == len(WIDE) - 1:
                        turn(nxt, 1)

        def post_wide(s, c, part, dest):
            buf = s % 2
            lo, hi = CHUNKS[c]
            mid = lo + (hi - lo + 1) // 2
            for u in range(lo, mid) if part == 0 else range(mid, hi):
                g, db = u // 4, u % 4
                f = pltpu.matmul_pop(wide[0][c % 2][u - lo]) + pltpu.matmul_pop(wide[1][c % 2][u - lo])
                low, high = [], []
                for i4 in range(4):
                    i = g * 4 + i4
                    v = (f[i4 * 16 : (i4 + 1) * 16, :] * ANG[s, i : i + 1, :]).astype(BF)
                    low.append(v[:, :128])
                    high.append(v[:, 128:])
                for base, xs in ((0, low), (4, high)):
                    for n, v in enumerate(swap_blocks((lane_f[0] < 0.5, lane_f[1] < 0.5), xs)):
                        OUT[buf, dest[base + n], db * 16 : (db + 1) * 16, g * 128 : (g + 1) * 128] = v

        def post_pair(s, j):
            buf = s % 2
            e, u = j // 4, (j // 2) % 2
            for m in range(2):
                nt = u * 2 + m
                f = pltpu.matmul_pop(narrow[m][j // 2])
                for h in range(2):
                    g = nt * 2 + h
                    v = f[:, h * 128 : (h + 1) * 128] * ANGP[s, e, g : g + 1, :]
                    OUT[buf, roles[s, 0, PAIR + e], :, g * 128 : (g + 1) * 128] = v.astype(BF)

        def copy(s):
            place = (s % 4) * 4 + ((s // 4) % 2) * 2 + s // 8
            return pltpu.make_async_copy(OUT.at[s % 2, pl.ds(0, CAP)], out.at[pl.ds(place * CAP, CAP)], sem.at[s % 2])

        turn(0, 0)
        turn(0, 1)
        push_wide(0)
        push_pair(0, 0)
        step(0, 0, 0)

        def sender(s, _):
            nxt = jnp.minimum(s + 1, NS - 1)
            dest = [roles[s, 0, DEST + n] for n in range(CAP)]

            @pl.when(s >= 2)
            def _():
                copy(s - 2).wait()

            for k in range(1, len(STEPS) + 1):
                if k < len(STEPS):
                    step(s, k, nxt)
                    what = STEPS[k]
                else:
                    step(nxt, 0, nxt)
                    what = (6, 0)
                if isinstance(what, int):
                    continue
                done = STEPS[k - 1]
                if isinstance(done, int) and done % 2 == 1 and k < len(STEPS):
                    post_pair(s, done)
                c = what[0]
                if c > 0:
                    first = not any(not isinstance(w, int) and w[0] == c for w in STEPS[:k])
                    post_wide(s, c - 1, 0 if first else 1, dest)
            post_wide(s, 5, 1, dest)
            copy(s).start()
            return 0

        lax.fori_loop(0, NS, sender, 0)
        left = jnp.zeros((64, 256), F32)
        for m in range(2):
            pltpu.matmul_acc_lhs(wide[m][0][0], kt_ref[:, halves(m)], load_staged_rhs=0)
            pltpu.matmul_acc_lhs(narrow[m][0], kt_ref[:, halves(m)], load_staged_rhs=1)
            for acc in (*wide[m][0], narrow[m][0]):
                left = left + pltpu.matmul_pop(acc)
        OUT[0, CAP, :, 0:256] = left.astype(BF)
        copy(NS - 2).wait()
        copy(NS - 1).wait()

    pl.run_scoped(whole, *[pltpu.ACC(m)((64, 256), F32) for m in range(2) for _ in range(16)])


def gather(wave, labels, rows, cols, owners, kt):
    vm = pl.BlockSpec(memory_space=pltpu.VMEM)
    blocks = pltpu.VMEM((2, 4, 4, 4, 16, 128), BF)
    i32 = jnp.int32
    dma = pltpu.SemaphoreType.DMA
    return pl.pallas_call(
        gather_kernel,
        in_specs=[pl.BlockSpec(memory_space=pltpu.HBM)] * 6,
        out_specs=[vm] * 5,
        out_shape=[
            jax.ShapeDtypeStruct((49, 32, 512), BF),
            jax.ShapeDtypeStruct((NS, 1, 128), i32),
            jax.ShapeDtypeStruct((NS, 32, 256), F32),
            jax.ShapeDtypeStruct((NS, 2, 8, 128), F32),
            jax.ShapeDtypeStruct((D, 512), BF),
        ],
        scratch_shapes=[
            blocks, blocks, blocks,
            pltpu.VMEM((2, 2, 4, 1, 128), i32),
            pltpu.VMEM((4, 4, 1, 128), i32),
            pltpu.VMEM((4, 4, 1, 128), i32),
            pltpu.VMEM((2, 4, 2, 1, 128), i32),
            pltpu.VMEM((64, 96), BF),
            pltpu.VMEM((1, 96), i32),
            pltpu.VMEM((1, 64), i32),
            pltpu.VMEM((1, 64), i32),
            pltpu.VMEM((1, 64), i32),
            dma((6,)),
            dma((3, 3)), dma((3, 4)), dma((3,)), dma((3, 3)), dma((3,)), dma((3,)),
        ],
        compiler_params=pltpu.CompilerParams(
            collective_id=0, has_side_effects=True, vmem_limit_bytes=24 * 2**20
        ),
    )(wave, labels, rows, cols, owners, kt)


def forms(roles, w_all, ang, ang_pair, kt):
    vm = pl.BlockSpec(memory_space=pltpu.VMEM)
    return pl.pallas_call(
        forms_kernel,
        in_specs=[pl.BlockSpec(memory_space=pltpu.SMEM), vm, vm, vm, vm],
        out_specs=pl.BlockSpec(memory_space=pltpu.HBM),
        out_shape=jax.ShapeDtypeStruct((NS * CAP, D, 1024), BF),
        scratch_shapes=[
            pltpu.VMEM((2, CAP + 1, D, 1024), BF),
            pltpu.VMEM((512, 256), BF),
            pltpu.VMEM((512, 256), BF),
            pltpu.SemaphoreType.DMA((2,)),
        ],
        compiler_params=pltpu.CompilerParams(vmem_limit_bytes=40 * 2**20),
    )(roles, w_all, ang, ang_pair, kt)


def per_device(wavefuncs, kernel, labels, row_tiles, col_tiles, owners):
    def in_hbm(v):
        return pltpu.with_memory_space_constraint(v, pltpu.HBM)

    w_all, roles, ang, ang_pair, kt = gather(
        in_hbm(wavefuncs.T),
        in_hbm(labels.reshape(1, 96)),
        in_hbm(row_tiles.reshape(1, 64)),
        in_hbm(col_tiles.reshape(1, 64)),
        in_hbm(owners.T),
        in_hbm(kernel.T),
    )
    return forms(roles, w_all, ang, ang_pair, kt)


def solution(mesh):
    return jax.shard_map(
        per_device,
        mesh=mesh,
        in_specs=(P("bin", "dist"), P(None, "dist"), P("bin"), P("bin"), P("bin"), P("bin", None)),
        out_specs=P("bin", "dist", None),
        check_vma=False,
    )
```

```python
import functools
import jax
import jax.numpy as jnp
from jax import lax
from jax.experimental import pallas as pl
from jax.experimental.pallas import tpu as pltpu
from jax.sharding import PartitionSpec as P

D = 64
RPT = 3
CAP = 8
NS = 16
BF = jnp.bfloat16
F32 = jnp.float32
MESH = pl.DeviceIdType.MESH


TILES, DEST, ROW, PAIR, PAIR_TILE = 0, 16, 24, 27, 29


def factor(li, lj):
    return jnp.sqrt((2.0 * li + 1.0) * (2.0 * lj + 1.0)) / (8.0 * (1.0 + jnp.abs(li - lj)))


def tables(meta, roles, ang, ang_pair):
    lane = lax.broadcasted_iota(jnp.int32, (NS, 128), 1)
    sender = lax.broadcasted_iota(jnp.int32, (NS, 128), 0)
    found = jnp.concatenate([meta[c, h, p] for c in range(2) for h in range(2) for p in range(4)], axis=0)
    ok = (found > 0) & (lane < CAP)
    at = jnp.maximum(found - 1, 0)
    row, tile = at >> 6, at & 63

    def total(mask, value):
        return jnp.sum(jnp.where(mask, value, 0), axis=1, keepdims=True)

    n = [total(ok & (row == r), 1) for r in range(RPT)]
    third = jnp.where((n[0] <= n[1]) & (n[0] <= n[2]), 0, jnp.where(n[1] <= n[2], 1, 2))
    first = jnp.where(third == 0, 1, 0)
    second = jnp.where(third == 2, 1, 2)
    single = ok & (row == third)
    p0 = jnp.min(jnp.where(single, lane, CAP), axis=1, keepdims=True)
    p1 = jnp.max(jnp.where(single, lane, -1), axis=1, keepdims=True)
    p1 = jnp.where((p1 == p0) | (p1 < 0), CAP, p1)
    t0 = jnp.where(p0 < CAP, total(single & (lane == p0), tile), 48)
    t1 = jnp.where(p1 < CAP, total(single & (lane == p1), tile), 48)
    role = jnp.where(ok & (row == first), tile, 48)
    role = jnp.where(lane < 8, role, pltpu.roll(jnp.where(ok & (row == second), tile, 48), 8, 1))
    role = jnp.where(lane < 16, role, pltpu.roll(jnp.where(single, CAP, lane), 16, 1))
    for k, v in enumerate((first * 16 + sender, second * 16 + sender, third * 16 + sender, p0, p1, t0, t1)):
        role = jnp.where(lane == ROW + k, v, role)
    for s in range(NS):
        roles[s] = role[s : s + 1, :]

    real = found.astype(F32)
    rolled = [real] + [pltpu.roll(real, 32 * k, 1) for k in (1, 2, 3)]
    labels = []
    for rt in range(RPT):
        v = rolled[(0 - rt - 1) % 4]
        for g in (1, 2, 3):
            v = jnp.where(lane // 32 == g, rolled[(g - rt - 1) % 4], v)
        labels.append(v)
    row_of = [jnp.take_along_axis(row, lane // 32 + 4 * h, axis=1) for h in range(2)]
    tile_of = [jnp.take_along_axis(tile, lane // 32 + 4 * h, axis=1) for h in range(2)]
    tile_of += [jnp.broadcast_to(t, (NS, 128)) for t in (t0, t1)]
    col = [jnp.zeros((NS, 128), F32) for _ in tile_of]
    for t in range(48):
        of = jnp.broadcast_to(labels[t // 16][t % 16 : t % 16 + 1, :], (NS, 128))
        col = [jnp.where(which == t, of, v) for which, v in zip(tile_of, col)]
    of_third = jnp.where(third == 0, labels[0], jnp.where(third == 1, labels[1], labels[2]))
    lane32 = lax.broadcasted_iota(jnp.int32, (32, 128), 1)
    eye = lane32 == lax.broadcasted_iota(jnp.int32, (32, 128), 0)
    spread = lax.broadcasted_iota(jnp.int32, (8, 128), 0) * 4 + lax.broadcasted_iota(jnp.int32, (8, 128), 1) // 32

    def line(v, s, rows):
        return jnp.broadcast_to(v[s : s + 1, :], (rows, 128))

    for s in range(NS):
        down = [jnp.sum(jnp.where(eye, line(labels[rt], s, 32), 0.0), axis=1, keepdims=True) for rt in range(RPT)]
        for h in range(2):
            r = line(row_of[h], s, 32)
            li = jnp.where(r == 0, down[0], jnp.where(r == 1, down[1], down[2]))
            ang[s, :, h * 128 : (h + 1) * 128] = factor(li, line(col[h], s, 32))
        li = jnp.take_along_axis(line(of_third, s, 8), spread, axis=1)
        for e in range(2):
            ang_pair[s, e] = factor(li, line(col[2 + e], s, 8))


def gather_kernel(wave_in, labels_in, rows_in, cols_in, owners_in, kt_in, w_all, roles, ang, ang_pair, kt,
                  b0, b1, b2, meta, table, via_x, via_y, wave, labels, rows, cols, owners, in_sem,
                  z_send, z_recv, c_send, c_recv, m_send, m_recv):
    loads = [
        pltpu.make_async_copy(src, dst, in_sem.at[k])
        for k, (src, dst) in enumerate(
            ((wave_in, wave), (labels_in, labels), (rows_in, rows), (cols_in, cols), (owners_in, owners), (kt_in, kt))
        )
    ]
    for load in loads:
        load.start()
    own, own_d = lax.axis_index("bin"), lax.axis_index("dist")
    x, yh, core = own // 4, (own // 2) % 2, own % 2
    z, yl = own_d // 2, own_d % 2
    y = yh * 2 + yl
    other = 1 - core

    def chip(px, py, pz, pc):
        return (px * 4 + (py // 2) * 2 + pc, pz * 2 + py % 2)

    def up(v, o):
        return (v + o) % 4

    def peer(axis, o):
        return chip(
            up(x, o) if axis == "x" else x, up(y, o) if axis == "y" else y, up(z, o) if axis == "z" else z, core
        )

    def diagonal(axis, o, axis2, o2):
        by = {axis: o, axis2: o2}
        return chip(up(x, by.get("x", 0)), up(y, by.get("y", 0)), up(z, by.get("z", 0)), core)

    barrier = pltpu.get_barrier_semaphore()
    peers = [peer(axis, o) for o in (2, 1, 3) for axis in "xyz"] + [chip(x, y, z, other)]
    peers += [diagonal(p, o, q, o2) for p, q in ("zy", "yx", "xz") for o in (2, 1, 3) for o2 in (2, 1, 3)]
    for at in peers:
        pl.semaphore_signal(barrier, inc=1, device_id=at, device_id_type=MESH)

    loads[0].wait()
    shard = wave[...].astype(F32).T
    for rt, b in enumerate((b0, b1, b2)):
        part = jnp.concatenate(
            [shard[rt * 32 : rt * 32 + 16, :], shard[rt * 32 + 16 : rt * 32 + 32, :]], axis=1
        ).astype(BF)
        if rt == 0:
            b[core, x, y, z] = part
        elif rt == 1:
            b[core, z, x, y] = part
        else:
            b[core, y, z, x] = part

    pl.semaphore_wait(barrier, len(peers))

    def copy(src, dst, send, recv, device):
        return pltpu.make_async_remote_copy(
            src_ref=src, dst_ref=dst, send_sem=send, recv_sem=recv, device_id=device, device_id_type=MESH
        )

    def taken(ref, send):
        copy(ref, ref, send, send, peers[0]).wait_send()

    def arrived(ref, recv):
        copy(ref, ref, recv, recv, peers[0]).wait_recv()

    def block(rt, stage, v, c):
        if rt == 0:
            return (b0.at[c, x, y, v], b0.at[c, x, v], b0.at[c, v])[stage]
        if rt == 1:
            return (b1.at[c, z, x, v], b1.at[c, z, v], b1.at[c, v])[stage]
        return (b2.at[c, y, z, v], b2.at[c, y, v], b2.at[c, v])[stage]

    def place(rt, stage):
        axis = ("zyx", "yxz", "xzy")[rt][stage]
        return {"x": x, "y": y, "z": z}[axis], axis

    def push(rt, stage):
        at, axis = place(rt, stage)
        mine = block(rt, stage, at, core)
        for o in (2, 1, 3):
            recv = z_recv.at[rt, stage + (stage == 2 and o == 2)]
            copy(mine, mine, z_send.at[rt, stage], recv, peer(axis, o)).start()

    def some(rt, stage, n):
        b = (b0, b1, b2)[rt]
        return (b.at[0, 0, 0, pl.ds(0, n)], b.at[0, 0, pl.ds(0, n)], b.at[0, pl.ds(0, n)])[stage]

    def across(rt, o, k):
        v = up(place(rt, 2)[0], (4 - o) % 4)
        copy(block(rt, 2, v, core), block(rt, 2, v, core), c_send.at[rt], c_recv.at[rt, k], chip(x, y, z, other)).start()

    def lay_stage(rt, c, o):
        if rt < 2:
            lay_plane(rt, up(place(rt, 2)[0], (4 - o) % 4), c)

    def lay(rt, c, px, h, pz, even, odd):
        tile = rt * 16 + c * 8 + h * 4 + px
        lanes = pl.ds(pl.multiple_of(pz * 128, 128), 128)
        w_all[tile, 0:16, lanes] = jnp.concatenate([even[:, :64], odd[:, :64]], axis=1)
        w_all[tile, 16:32, lanes] = jnp.concatenate([even[:, 64:], odd[:, 64:]], axis=1)

    def lay_plane(rt, v, c):
        if rt == 0:
            for h in range(2):
                for pz in range(4):
                    lay(0, c, v, h, pz, b0[c, v, 2 * h, pz], b0[c, v, 2 * h + 1, pz])
        elif rt == 1:
            for px in range(4):
                for h in range(2):
                    lay(1, c, px, h, v, b1[c, v, px, 2 * h], b1[c, v, px, 2 * h + 1])
        else:
            for pz in range(4):
                for px in range(4):
                    lay(2, c, px, v, pz, b2[c, 2 * v, pz, px], b2[c, 2 * v + 1, pz, px])

    for o, o2 in [(a, b) for a in (2, 1, 3, 0) for b in (2, 1, 3, 0) if a or b]:
        for rt, (p, q) in enumerate(("zy", "yx", "xz")):
            mine = block(rt, 0, place(rt, 0)[0], core)
            copy(mine, mine, z_send.at[rt, 0], z_recv.at[rt, 1 if o2 else 0], diagonal(p, o, q, o2)).start()

    for load in loads[1:]:
        load.wait()
    sub64 = lax.broadcasted_iota(jnp.int32, (64, 64), 0)
    lan64 = lax.broadcasted_iota(jnp.int32, (64, 64), 1)

    def column(row):
        return jnp.sum(jnp.where(sub64 == lan64, jnp.broadcast_to(row, (64, 64)), 0), axis=1, keepdims=True)

    own_r, col_r = owners[...], cols[...]
    own_c = column(own_r)
    same = (jnp.broadcast_to(own_c, (64, 64)) == own_r) & (lan64 < sub64)
    slot_c = jnp.sum(jnp.where(same, 1, 0), axis=1, keepdims=True)
    third = lax.shift_right_logical(col_r * 171, 9)
    number = (third & 1) * 8 + (third & 2) * 2 + lax.shift_right_logical(third, 2)
    code_c = column(1 + rows[...] * 64 + (col_r - 3 * third) * 16 + number)
    lane64 = lax.broadcasted_iota(jnp.int32, (64, 128), 1)
    lane1 = lax.broadcasted_iota(jnp.int32, (1, 128), 1)
    spread = jnp.where(lane64 == slot_c, jnp.broadcast_to(code_c, (64, 128)), 0)
    label_row = jnp.concatenate([jnp.zeros((1, 32), jnp.int32), labels[...]], axis=1)
    for o in range(NS):
        mine = jnp.where(own_c == o, spread, 0)
        table[o // 4, o % 4] = jnp.where(lane1 < 32, jnp.sum(mine, axis=0, keepdims=True), label_row)

    for o in (2, 1, 3):
        copy(table.at[up(x, o)], via_x.at[x], m_send.at[0], m_recv.at[0], peer("x", o)).start()
    via_x[x] = table[x]


    arrived(via_x.at[pl.ds(0, 3)], m_recv.at[0])
    taken(table.at[pl.ds(0, 3)], m_send.at[0])
    far = 1 - yh
    meta_y = copy(via_x.at[:, pl.ds(far * 2, 2)], via_y.at[yh], m_send.at[1], m_recv.at[1], peer("y", 2))
    meta_y.start()
    via_y[yh] = via_x[:, pl.ds(yh * 2, 2)]

    for rt in range(RPT):
        arrived(some(rt, 0, 3), z_recv.at[rt, 0])
        arrived(some(rt, 1, 3), z_recv.at[rt, 1])
        push(rt, 2)
        across(rt, 0, 0)
    for rt in range(RPT):
        taken(some(rt, 0, 3), z_send.at[rt, 0])
        taken(some(rt, 1, 3), z_send.at[rt, 0])

    arrived(via_y.at[far], m_recv.at[1])
    meta_c = copy(via_y.at[:, :, other], meta.at[core], m_send.at[2], m_recv.at[2], chip(x, y, z, other))
    meta_c.start()
    meta_y.wait_send()
    meta[core] = via_y[:, :, core]
    w_all[48] = jnp.zeros((32, 512), BF)
    lay_plane(0, x, core)
    lay_plane(1, z, core)

    arrived(meta.at[other], m_recv.at[2])
    meta_c.wait_send()
    tables(meta, roles, ang, ang_pair)
    for rt in range(RPT):
        arrived(some(rt, 2, 2), z_recv.at[rt, 2])
        across(rt, 1, 1)
        across(rt, 3, 1)
    for rt in range(RPT):
        arrived(some(rt, 2, 1), c_recv.at[rt, 0])
        lay_stage(rt, other, 0)
        lay_stage(rt, core, 1)
        lay_stage(rt, core, 3)
    lay_plane(2, yh, core)
    for rt in range(RPT):
        arrived(some(rt, 2, 1), z_recv.at[rt, 3])
        across(rt, 2, 2)
    for rt in range(RPT):
        arrived(some(rt, 2, 2), c_recv.at[rt, 1])
        lay_stage(rt, other, 1)
        lay_stage(rt, other, 3)
        lay_stage(rt, core, 2)
    lay_plane(2, yh, other)
    lay_plane(2, far, core)
    for rt in range(RPT):
        taken(some(rt, 2, 3), z_send.at[rt, 2])
    for rt in range(RPT):
        arrived(some(rt, 2, 1), c_recv.at[rt, 2])
        lay_stage(rt, other, 2)
    lay_plane(2, far, other)
    for rt in range(RPT):
        taken(some(rt, 2, 4), c_send.at[rt])


def swap_blocks(lane, x):
    half, even = lane

    def mixed(a, b, c, d):
        ab, cd = jnp.where(even, a, b), jnp.where(even, c, d)
        return jnp.where(half, ab, cd), jnp.where(half, cd, ab)

    z0, z2 = mixed(x[0], x[1], x[2], x[3])
    z1, z3 = mixed(x[3], x[0], x[1], x[2])
    u = z0, pltpu.roll(z1, 96, 1), pltpu.roll(z2, 64, 1), pltpu.roll(z3, 32, 1)
    y0, y2 = mixed(u[0], u[3], u[2], u[1])
    y1, y3 = mixed(u[1], u[0], u[3], u[2])
    return y0, y1, y2, y3


CHUNKS = ((0, 6), (6, 12), (12, 16))
WEIGHTS = ((0, 0), (0, 1), (1, 0), (1, 1))
STEPS = []
for c, order in enumerate((WEIGHTS, WEIGHTS[::-1], WEIGHTS)):
    for n, weights in enumerate(order):
        STEPS.append((c, *weights))
        piece = c * 3 + n
        if n < 3 and piece < 8:
            STEPS.append(piece)


def loads_weights(k):
    return k == 0 or isinstance(STEPS[k], int) or isinstance(STEPS[k - 1], int) or STEPS[k][1:] != STEPS[k - 1][1:]


WIDE = [k for k, step in enumerate(STEPS) if not isinstance(step, int) and loads_weights(k)]


def forms_kernel(roles, W, ANG, ANGP, kt_ref, out, OUT, cols_first, cols_second, sem):
    place = lax.broadcasted_iota(jnp.int32, (16, 128), 1) // 32
    lane_f = (place // 2).astype(F32).astype(BF), (place % 2).astype(F32).astype(BF)
    def halves(m):
        return slice(m * 256, (m + 1) * 256)

    def turn(s, which):
        cols = jnp.concatenate([W[roles[s, 0, TILES + 8 * which + n]] for n in range(CAP)], axis=0)
        (cols_first, cols_second)[which][...] = cols.T

    def push_wide(which, kh):
        for m in range(2):
            pltpu.matmul_push_rhs((cols_first, cols_second)[which][halves(kh), :], 0, m)

    def push_pair(s, j):
        e, u, kh = j // 4, (j // 2) % 2, j % 2
        rows = W.at[roles[s, 0, ROW + 2]]
        cols = W[roles[s, 0, PAIR_TILE + e], :, halves(kh)]
        for m in range(2):
            at = (u * 2 + m) * 8
            pair = jnp.concatenate([rows[i : i + 1, halves(kh)] * cols for i in range(at, at + 8)], axis=0)
            pltpu.matmul_push_rhs(pair, 1, m, transpose=True)

    def whole(*flat):
        wide = [[flat[m * 16 + b * 6 : m * 16 + b * 6 + 6] for b in range(2)] for m in range(2)]
        narrow = [flat[m * 16 + 12 : m * 16 + 16] for m in range(2)]

        def step(s, buf, k, nxt):
            what = STEPS[k]
            if isinstance(what, int):
                kh = what % 2
                for m in range(2):
                    pltpu.matmul_acc_lhs(narrow[m][what // 2], kt_ref[:, halves(kh)], load_staged_rhs=1)
                push_pair(s if what < 7 else nxt, (what + 1) % 8)
                return
            c, which, kh = what
            row = roles[s, 0, ROW + which]
            lo, hi = CHUNKS[c]
            for v in range(lo, hi):
                g = v // 2
                if v == lo or v % 2 == 0:
                    wide_rows = [
                        jnp.broadcast_to(W[row, i : i + 1, halves(kh)], (16, 256)) for i in range(g * 4, g * 4 + 4)
                    ]
                load = v == lo and loads_weights(k)
                for m in range(2):
                    db = 2 * m + v % 2
                    kt = kt_ref[db * 16 : (db + 1) * 16, halves(kh)]
                    lhs = jnp.concatenate([r * kt for r in wide_rows], axis=0)
                    acc = wide[m][(3 * buf + c) % 2][v - lo]
                    pltpu.matmul_acc_lhs(acc, lhs, load_staged_rhs=0 if load else None)
                if load:
                    at = WIDE.index(k) + 1
                    coming = STEPS[WIDE[at % len(WIDE)]][1:]
                    push_wide(*coming)
                    if at < len(WIDE) and not any(STEPS[j][1] == coming[0] for j in WIDE[at + 1 :]):
                        turn(nxt, coming[0])

        def post_wide(s, buf, c, part, dest):
            lo, hi = CHUNKS[c]
            mid = lo + (hi - lo + 1) // 2
            for v in range(lo, mid) if part == 0 else range(mid, hi):
                for m in range(2):
                    g, db = v // 2, 2 * m + v % 2
                    f = pltpu.matmul_pop(wide[m][(3 * buf + c) % 2][v - lo])
                    low, high = [], []
                    for i4 in range(4):
                        i = g * 4 + i4
                        x = (f[i4 * 16 : (i4 + 1) * 16, :] * ANG[s, i : i + 1, :]).astype(BF)
                        low.append(x[:, :128])
                        high.append(x[:, 128:])
                    for base, xs in ((0, low), (4, high)):
                        for n, y in enumerate(swap_blocks((lane_f[0] < 0.5, lane_f[1] < 0.5), xs)):
                            OUT[buf, dest[base + n], db * 16 : (db + 1) * 16, g * 128 : (g + 1) * 128] = y

        def post_pair(s, buf, j):
            e, u = j // 4, (j // 2) % 2
            for m in range(2):
                nt = u * 2 + m
                f = pltpu.matmul_pop(narrow[m][j // 2])
                for h in range(2):
                    g = nt * 2 + h
                    v = f[:, h * 128 : (h + 1) * 128] * ANGP[s, e, g : g + 1, :]
                    OUT[buf, roles[s, 0, PAIR + e], :, g * 128 : (g + 1) * 128] = v.astype(BF)

        def copy(s, buf):
            place = (s % 4) * 4 + ((s // 4) % 2) * 2 + s // 8
            return pltpu.make_async_copy(OUT.at[buf, pl.ds(0, CAP)], out.at[pl.ds(place * CAP, CAP)], sem.at[buf])

        turn(0, 0)
        turn(0, 1)
        push_wide(0, 0)
        push_pair(0, 0)
        step(0, 0, 0, 0)

        def sender(s, buf):
            nxt = jnp.minimum(s + 1, NS - 1)
            dest = [roles[s, 0, DEST + n] for n in range(CAP)]

            @pl.when(s >= 2)
            def _():
                copy(s - 2, buf).wait()

            for k in range(1, len(STEPS) + 1):
                if k < len(STEPS):
                    step(s, buf, k, nxt)
                    what = STEPS[k]
                else:
                    step(nxt, 1 - buf, 0, nxt)
                    what = (len(CHUNKS), 0, 0)
                if isinstance(what, int):
                    continue
                done = STEPS[k - 1]
                if isinstance(done, int) and done % 2 == 1 and k < len(STEPS):
                    post_pair(s, buf, done)
                c = what[0]
                if c > 0:
                    n = sum(not isinstance(w, int) and w[0] == c for w in STEPS[:k])
                    if n < 2:
                        post_wide(s, buf, c - 1, n, dest)
            post_wide(s, buf, len(CHUNKS) - 1, 1, dest)
            copy(s, buf).start()

        def two(t, _):
            sender(2 * t, 0)
            sender(2 * t + 1, 1)
            return 0

        lax.fori_loop(0, NS // 2, two, 0)
        left = jnp.zeros((64, 256), F32)
        for m in range(2):
            pltpu.matmul_acc_lhs(wide[m][0][0], kt_ref[:, halves(m)], load_staged_rhs=0)
            pltpu.matmul_acc_lhs(narrow[m][0], kt_ref[:, halves(m)], load_staged_rhs=1)
            for acc in (*wide[m][0], narrow[m][0]):
                left = left + pltpu.matmul_pop(acc)
        OUT[0, CAP, :, 0:256] = left.astype(BF)
        copy(NS - 2, 0).wait()
        copy(NS - 1, 1).wait()

    pl.run_scoped(whole, *[pltpu.ACC(m)((64, 256), F32) for m in range(2) for _ in range(16)])


def gather(wave, labels, rows, cols, owners, kt):
    vm = pl.BlockSpec(memory_space=pltpu.VMEM)
    blocks = pltpu.VMEM((2, 4, 4, 4, 16, 128), BF)
    i32 = jnp.int32
    dma = pltpu.SemaphoreType.DMA
    return pl.pallas_call(
        gather_kernel,
        in_specs=[pl.BlockSpec(memory_space=pltpu.HBM)] * 6,
        out_specs=[vm] * 5,
        out_shape=[
            jax.ShapeDtypeStruct((49, 32, 512), BF),
            jax.ShapeDtypeStruct((NS, 1, 128), i32),
            jax.ShapeDtypeStruct((NS, 32, 256), F32),
            jax.ShapeDtypeStruct((NS, 2, 8, 128), F32),
            jax.ShapeDtypeStruct((D, 512), BF),
        ],
        scratch_shapes=[
            blocks, blocks, blocks,
            pltpu.VMEM((2, 2, 4, 1, 128), i32),
            pltpu.VMEM((4, 4, 1, 128), i32),
            pltpu.VMEM((4, 4, 1, 128), i32),
            pltpu.VMEM((2, 4, 2, 1, 128), i32),
            pltpu.VMEM((64, 96), BF),
            pltpu.VMEM((1, 96), i32),
            pltpu.VMEM((1, 64), i32),
            pltpu.VMEM((1, 64), i32),
            pltpu.VMEM((1, 64), i32),
            dma((6,)),
            dma((3, 3)), dma((3, 4)), dma((3,)), dma((3, 3)), dma((3,)), dma((3,)),
        ],
        compiler_params=pltpu.CompilerParams(
            collective_id=0, has_side_effects=True, vmem_limit_bytes=24 * 2**20
        ),
    )(wave, labels, rows, cols, owners, kt)


def forms(roles, w_all, ang, ang_pair, kt):
    vm = pl.BlockSpec(memory_space=pltpu.VMEM)
    return pl.pallas_call(
        forms_kernel,
        in_specs=[pl.BlockSpec(memory_space=pltpu.SMEM), vm, vm, vm, vm],
        out_specs=pl.BlockSpec(memory_space=pltpu.HBM),
        out_shape=jax.ShapeDtypeStruct((NS * CAP, D, 1024), BF),
        scratch_shapes=[
            pltpu.VMEM((2, CAP + 1, D, 1024), BF),
            pltpu.VMEM((512, 256), BF),
            pltpu.VMEM((512, 256), BF),
            pltpu.SemaphoreType.DMA((2,)),
        ],
        compiler_params=pltpu.CompilerParams(vmem_limit_bytes=40 * 2**20),
    )(roles, w_all, ang, ang_pair, kt)


def per_device(wavefuncs, kernel, labels, row_tiles, col_tiles, owners):
    def in_hbm(v):
        return pltpu.with_memory_space_constraint(v, pltpu.HBM)

    w_all, roles, ang, ang_pair, kt = gather(
        in_hbm(wavefuncs.T),
        in_hbm(labels.reshape(1, 96)),
        in_hbm(row_tiles.reshape(1, 64)),
        in_hbm(col_tiles.reshape(1, 64)),
        in_hbm(owners.T),
        in_hbm(kernel.T),
    )
    return forms(roles, w_all, ang, ang_pair, kt)


def solution(mesh):
    return jax.shard_map(
        per_device,
        mesh=mesh,
        in_specs=(P("bin", "dist"), P(None, "dist"), P("bin"), P("bin"), P("bin"), P("bin", None)),
        out_specs=P("bin", "dist", None),
        check_vma=False,
    )
```
